32 devices in a mesh: rcv: 8 (over z, y), hd: 4 (over x, core).
Axes of the slice: x: 2, y: 2, z: 4, core: 2. Of those that a mesh axis runs over, the one named last changes fastest.
Arguments:
- stream: bfloat16 [4096, 1024], P(('rcv', 'hd')), may hold values from -3 to 3
- queries: bfloat16 [4096, 1024], P(('rcv', 'hd')), may hold values from -9 to 9
- keys: bfloat16 [4096, 1024], P(('rcv', 'hd')), may hold values from -9 to 9
- values: bfloat16 [4096, 1024], P(('rcv', 'hd')), may hold values from -6 to 6
- out_proj: bfloat16 [1024, 1024], replicated, may hold values from -0.375 to 0.375
- norm_gain: float32 [1024], replicated, may hold values from 0.5 to 1.5
- expert_weights: bfloat16 [1024, 16, 3, 512], P(None, 'rcv'), may hold values from -0.1875 to 0.1875
- expert_ids: int32 [4096, 4], P(('rcv', 'hd')), may hold values from 0 to 15, as said below
- gate_weights: float32 [4096, 4], P(('rcv', 'hd')), may hold values from 0.1 to 1
- out_cotangent: bfloat16 [4096, 1024], P(('rcv', 'hd')), may hold values from -6 to 6
Outputs:
- block_out: bfloat16 [4096, 1024], P(('rcv', 'hd'))
- stream_grad: bfloat16 [4096, 1024], P(('rcv', 'hd'))
The draws below stay inside these ranges and needn't reach their ends.
Inputs may be any that keep to these rules, and one draw needn't show every extreme that they name: `expert_ids`: each token names 4 different experts; its k-th id lies in k * 4 to (k + 1) * 4 - 1. Within each aligned block of 128 rows no expert is named more than 40 times, and in each of these 4 ranges one expert, the same for all blocks, is named exactly 40 times in every block.
All inputs are finite; a program needn't handle non-finite values.
Results may differ from the reference program's by a relative error of at most 0.015.
Values may be sent and summed in bfloat16 or wider, within the bound.
No kernel may reach another device: no remote copies, remote signals or barrier semaphores. Data moves between devices by JAX's collectives and lax.ppermute only.
A program may use at most 128 MiB of HBM per device.

```python
import math
import jax
import jax.numpy as jnp
from jax import lax

D = 1024
HEADS = 16
HS = 64
FF = 512
TOPK = 4
TOK_DEV = 128
EXPERTS = 16
CAP = 40
TOKENS = 4096
N_HD = 4


def query_key_pair(key):
    base_key = jax.random.fold_in(key, 11)
    query_key, key_key = jax.random.split(base_key, 2)
    query_draw = jnp.clip(1.5 * jax.random.normal(query_key, (TOKENS, D), jnp.float32), -9.0, 9.0)
    key_draw = jnp.clip(1.5 * jax.random.normal(key_key, (TOKENS, D), jnp.float32), -9.0, 9.0)
    return (query_draw, key_draw)


def draw_queries(key, part):
    return query_key_pair(key)[0].astype(jnp.bfloat16)


def draw_keys(key, part):
    return query_key_pair(key)[1].astype(jnp.bfloat16)


def draw_expert_ids(key, part):
    block_count = TOKENS // TOK_DEV
    group_size = EXPERTS // TOPK
    hot_key, cell_key = jax.random.split(jax.random.fold_in(key, 5), 2)
    hot_expert = jax.random.randint(hot_key, (TOPK,), 0, group_size)
    offsets = jnp.arange(group_size - 1, dtype=jnp.int32)

    def one_block(block_key):
        first_key, second_key = jax.random.split(block_key)
        columns = []
        for column in range(TOPK):
            others = (hot_expert[column] + 1 + offsets) % group_size
            cell_list = jax.random.permutation(jax.random.fold_in(first_key, column), jnp.repeat(others, CAP))
            sequence = jnp.concatenate([jnp.full((CAP,), hot_expert[column], jnp.int32), cell_list.astype(jnp.int32)])[:TOK_DEV]
            sequence = jax.random.permutation(jax.random.fold_in(second_key, column), sequence)
            columns.append(sequence + column * group_size)
        return jnp.stack(columns, axis=1)
    block_keys = jax.random.split(cell_key, block_count)
    return jax.vmap(one_block)(block_keys).reshape(TOKENS, TOPK).astype(jnp.int32)


def steps_of(stream_key, shape, pieces, least, top_value):
    level, own = 1.0, jax.random.fold_in(stream_key, 6)
    for axis_at, parts in pieces:
        heights = jnp.exp(jax.random.uniform(jax.random.fold_in(own, axis_at), (parts,), jnp.float32, least / len(pieces), top_value / len(pieces)))
        level = level * jnp.repeat(heights, shape[axis_at] // parts).reshape([-1 if axis == axis_at else 1 for axis in range(len(shape))])
    return level


def normal_values(key, extent, spread, bound, cuts=(), kind=jnp.bfloat16):
    values = spread * jax.random.normal(key, extent, jnp.float32)
    if cuts:
        values = values * steps_of(key, extent, cuts, -0.22, 0.18)
    return jnp.clip(values, -bound, bound).astype(kind)


def setup_inputs(seed: int = 0) -> dict:
    seeds = jax.random.split(jax.random.key(seed), 11)
    return {
        "stream": normal_values(seeds[0], (TOKENS, D), 0.5, 3.0, ((0, 32),)),
        "queries": draw_queries(jax.random.fold_in(seeds[10], 71), 0),
        "keys": draw_keys(jax.random.fold_in(seeds[10], 71), 0),
        "values": normal_values(seeds[3], (TOKENS, D), 1.0, 6.0, ((0, 32),)),
        "out_proj": normal_values(seeds[4], (D, D), (D // 4) ** -0.5, 0.375),
        "norm_gain": jnp.clip(1.0 + 0.1 * jax.random.normal(seeds[5], (D,), jnp.float32), 0.5, 1.5),
        "expert_weights": normal_values(seeds[6], (D, EXPERTS, 3, FF), D ** -0.5, 0.1875, ((1, 8),)),
        "expert_ids": draw_expert_ids(jax.random.fold_in(seeds[10], 71), 0),
        "gate_weights": jnp.clip(jnp.exp(math.log(1.0) - 2.3025851 * jax.random.uniform(seeds[8], (TOKENS, TOPK), jnp.float32) ** steps_of(seeds[8], (TOKENS, TOPK), ((0, 32),), -0.2, 0.2)), 0.1, 1.0),
        "out_cotangent": normal_values(seeds[9], (TOKENS, D), 1.0, 6.0, ((0, 32),)),
    }


NORM_EPS = 1e-06

def silu_parts(pre_gate):
    sigmoid = 1.0 / (1.0 + jnp.exp(-pre_gate))
    return (pre_gate * sigmoid, sigmoid * (1.0 + pre_gate * (1.0 - sigmoid)))

def attend_sequence(query_rows, key_rows, value_rows):
    length = query_rows.shape[0]
    query_heads = query_rows.reshape(length, HEADS, HS).astype(jnp.float32)
    key_heads = key_rows.reshape(length, HEADS, HS).astype(jnp.float32)
    value_heads = value_rows.reshape(length, HEADS, HS).astype(jnp.float32)
    scores = jnp.einsum('qhd,khd->hqk', query_heads, key_heads) * (1.0 / math.sqrt(HS))
    row_max = lax.optimization_barrier(jnp.max(scores, axis=2, keepdims=True))
    raw_weights = jnp.exp(scores - row_max)
    row_total = lax.optimization_barrier(jnp.sum(raw_weights, axis=2))
    rounded = raw_weights.astype(jnp.bfloat16).astype(jnp.float32)
    mixed_heads = jnp.einsum('hqk,khd->qhd', rounded, value_heads)
    result = mixed_heads / jnp.transpose(row_total)[:, :, None]
    return result.astype(jnp.bfloat16).reshape(length, HEADS * HS)

def expert_reference(cell_inputs, cell_cots, weight_block):
    gate_up = weight_block[:, :2].astype(jnp.float32)
    down_t = weight_block[:, 2].astype(jnp.float32)
    pre_pair = jnp.einsum('md,dcf->mcf', cell_inputs.astype(jnp.float32), gate_up)
    activated, act_slope = silu_parts(pre_pair[:, 0])
    up_value = pre_pair[:, 1]
    hidden = (activated * up_value).astype(jnp.bfloat16)
    expert_outs = jnp.einsum('mf,df->md', hidden.astype(jnp.float32), down_t).astype(jnp.bfloat16)
    back_hidden = jnp.einsum('md,df->mf', cell_cots.astype(jnp.float32), down_t)
    hidden_grads = jnp.stack([back_hidden * up_value * act_slope, back_hidden * activated], axis=1).astype(jnp.bfloat16)
    expert_grads = jnp.einsum('mcf,dcf->md', hidden_grads.astype(jnp.float32), gate_up).astype(jnp.bfloat16)
    return (expert_outs, expert_grads)

def reference(stream, queries, keys, values, out_proj, norm_gain, expert_weights, expert_ids, gate_weights, out_cotangent):
    length = TOK_DEV * N_HD
    seq_count = TOKENS // length

    def one_sequence(seq_index):
        row_start = seq_index * length
        return attend_sequence(lax.dynamic_slice_in_dim(queries, row_start, length, 0), lax.dynamic_slice_in_dim(keys, row_start, length, 0), lax.dynamic_slice_in_dim(values, row_start, length, 0))
    attended = lax.map(one_sequence, jnp.arange(seq_count, dtype=jnp.int32)).reshape(TOKENS, D)
    projected = jnp.dot(attended, out_proj, preferred_element_type=jnp.float32)
    mix_stream = (stream.astype(jnp.float32) + projected).astype(jnp.bfloat16)
    stream_wide = mix_stream.astype(jnp.float32)
    inverse = lax.rsqrt(lax.optimization_barrier(jnp.mean(stream_wide * stream_wide, axis=1, keepdims=True)) + NORM_EPS)
    normed = (norm_gain * stream_wide * inverse).astype(jnp.bfloat16)
    block_count = TOKENS // TOK_DEV
    block_ids = expert_ids.reshape(block_count, TOK_DEV * TOPK)
    onehot = (block_ids[:, :, None] == jnp.arange(EXPERTS, dtype=jnp.int32)[None, None, :]).astype(jnp.int32)
    slot_index = lax.optimization_barrier(jnp.sum((jnp.cumsum(onehot, axis=1) - onehot) * onehot, axis=2))
    block_index = jnp.arange(block_count, dtype=jnp.int32)[:, None]
    position = (block_index * CAP + slot_index).reshape(-1).astype(jnp.int32)
    flat_ids = expert_ids.reshape(-1).astype(jnp.int32)
    token_index = jnp.arange(TOKENS * TOPK, dtype=jnp.int32) // TOPK
    source = jnp.full((EXPERTS, block_count * CAP), TOKENS, jnp.int32).at[flat_ids, position].set(token_index)
    gate_table = jnp.zeros((EXPERTS, block_count * CAP), jnp.float32).at[flat_ids, position].set(gate_weights.reshape(-1))
    normed_pad = jnp.concatenate([normed, jnp.zeros((1, D), jnp.bfloat16)], axis=0)
    cot_pad = jnp.concatenate([out_cotangent, jnp.zeros((1, D), jnp.bfloat16)], axis=0)
    weights_major = jnp.moveaxis(expert_weights, 1, 0)

    def expert_step(running, expert_item):
        out_accum, grad_accum = running
        cell_rows, gate_column, weight_block = expert_item
        expert_outs, expert_grads = expert_reference(jnp.take(normed_pad, cell_rows, axis=0), jnp.take(cot_pad, cell_rows, axis=0), weight_block)
        out_accum = out_accum.at[cell_rows].add(gate_column[:, None] * expert_outs.astype(jnp.float32))
        grad_accum = grad_accum.at[cell_rows].add(gate_column[:, None] * expert_grads.astype(jnp.float32))
        return ((out_accum, grad_accum), None)
    start_state = (jnp.zeros((TOKENS + 1, D), jnp.float32), jnp.zeros((TOKENS + 1, D), jnp.float32))
    (out_accum, grad_accum), _ = lax.scan(expert_step, start_state, (source, gate_table, weights_major))
    block_out = (stream_wide + out_accum[:TOKENS]).astype(jnp.bfloat16)
    weighted = norm_gain * grad_accum[:TOKENS]
    scaled = stream_wide * inverse
    stream_grad = out_cotangent.astype(jnp.float32) + inverse * (weighted - scaled * lax.optimization_barrier(jnp.mean(weighted * scaled, axis=1, keepdims=True)))
    return (block_out, stream_grad.astype(jnp.bfloat16))
```

```python
import functools
import math

import jax
import jax.numpy as jnp
from jax import lax
from jax.experimental import pallas as pl
from jax.experimental.pallas import tpu as pltpu
from jax.sharding import PartitionSpec as P

HS = 64
LANES = 128
CHUNK = 32
NORM_EPS = 1e-06
VMEM_BYTES = 48 << 20
F32, BF16 = jnp.float32, jnp.bfloat16


def dot(a, b, contract=((1,), (0,))):
    return lax.dot_general(a, b, (contract, ((), ())), preferred_element_type=F32)


def params():
    return pltpu.CompilerParams(vmem_limit_bytes=VMEM_BYTES)


def vmem_specs(count):
    return [pl.BlockSpec(memory_space=pltpu.VMEM)] * count


def cost(flops, nbytes):
    return pl.CostEstimate(flops=int(flops), bytes_accessed=int(nbytes), transcendentals=0)


def split_kernel(w_ref, o_ref):
    for part in range(w_ref.shape[1]):
        by_expert = jnp.swapaxes(w_ref[:, part], 0, 1)
        for block in range(o_ref.shape[0]):
            for expert in range(by_expert.shape[0]):
                o_ref[block, expert, part] = by_expert[expert, block * CHUNK : (block + 1) * CHUNK]


def split_experts(expert_weights):
    depth, local, parts, hidden = expert_weights.shape
    rows = 4 * CHUNK
    return pl.pallas_call(
        split_kernel,
        grid=(depth // rows,),
        in_specs=[pl.BlockSpec((rows, parts, local, hidden), lambda i: (i, 0, 0, 0))],
        out_specs=pl.BlockSpec((4, local, parts, CHUNK, hidden), lambda i: (i, 0, 0, 0, 0)),
        out_shape=jax.ShapeDtypeStruct((depth // CHUNK, local, parts, CHUNK, hidden), BF16),
        compiler_params=params(),
        cost_estimate=cost(0, 4 * depth * local * parts * hidden),
        name="split_experts",
    )(jnp.transpose(expert_weights, (0, 2, 1, 3)))


def attention_kernel(count, q_ref, stream_ref, proj_ref, gain_ref, *refs):
    kv_refs, (mix_ref, normed_ref, attended) = refs[:count], refs[count:]
    rows, width = q_ref.shape
    first = lax.broadcasted_iota(jnp.int32, (rows, LANES), 1) < HS
    for pair in range(width // LANES):
        cols = slice(pair * LANES, (pair + 1) * LANES)
        query = q_ref[:, cols] * jnp.asarray(1.0 / math.sqrt(HS), BF16)
        zero = jnp.zeros_like(query)
        both = jnp.concatenate([jnp.where(first, query, zero), jnp.where(first, zero, query)], axis=0)
        keys = jnp.concatenate([r[:rows, cols] for r in kv_refs], axis=0)
        vals = jnp.concatenate([r[rows:, cols] for r in kv_refs], axis=0)
        scores = dot(both, keys, ((1,), (1,)))
        raw = jnp.exp(scores - jnp.max(scores, axis=1, keepdims=True))
        total = jnp.sum(raw, axis=1, keepdims=True)
        mixed = dot(raw.astype(BF16), vals) / total
        attended[:, cols] = jnp.where(first, mixed[:rows], mixed[rows:]).astype(BF16)
    mix = (stream_ref[...].astype(F32) + dot(attended[...], proj_ref[...])).astype(BF16)
    mix_ref[...] = mix
    wide = mix.astype(F32)
    inverse = lax.rsqrt(jnp.mean(wide * wide, axis=1, keepdims=True) + NORM_EPS)
    normed_ref[...] = (gain_ref[...] * wide * inverse).astype(BF16)


def attention(queries, stream, out_proj, norm_gain, kv_blocks):
    shape = jax.ShapeDtypeStruct(stream.shape, BF16)
    rows, width = stream.shape
    return pl.pallas_call(
        functools.partial(attention_kernel, len(kv_blocks)),
        in_specs=vmem_specs(4 + len(kv_blocks)),
        out_specs=vmem_specs(2),
        out_shape=(shape, shape),
        scratch_shapes=[pltpu.VMEM(stream.shape, BF16)],
        compiler_params=params(),
        cost_estimate=cost(8e9, 4e6),
        name="attention",
    )(queries, stream, out_proj, norm_gain[None, :], *kv_blocks)


def pick_rows(where_ref, meta_refs, experts, slots):
    choice, member = where_ref[0], where_ref[1]
    rows = meta_refs[0].shape[1]
    names, gates = [], []
    for ref in meta_refs:
        meta = ref[...].astype(F32)
        top = meta.shape[0] // 4
        line = lax.broadcasted_iota(jnp.int32, meta.shape, 0)
        names.append(jnp.sum(jnp.where(line == choice, meta, 0.0), axis=0, keepdims=True))
        gate = jnp.where((line >= top) & (lax.rem(line, top) == choice), meta, 0.0)
        gate = jnp.broadcast_to(jnp.sum(gate, axis=0, keepdims=True), (rows, rows))
        gates.append(jnp.transpose(gate)[:, :1])
    names = jnp.concatenate(names, axis=1)
    count = names.shape[1]
    named = names.astype(jnp.int32) - choice * experts
    lines = max(experts, 8)
    chosen = named == lax.broadcasted_iota(jnp.int32, (lines, count), 0)
    earlier = lax.broadcasted_iota(jnp.int32, (count, count), 0) < lax.broadcasted_iota(
        jnp.int32, (count, count), 1
    )
    ones = jnp.where(chosen, 1.0, 0.0).astype(BF16)
    rank = dot(ones, jnp.where(earlier, 1.0, 0.0).astype(BF16))
    own_rank = jnp.sum(jnp.where(chosen, rank, 0.0), axis=0, keepdims=True).astype(jnp.int32)

    def matrix(expert):
        target = jnp.where(named == expert, own_rank, -1)
        hit = target == lax.broadcasted_iota(jnp.int32, (slots, count), 0)
        return jnp.where(hit, 1.0, 0.0).astype(BF16)

    return matrix, gates


def weight_copies(where_ref, sets, buffer, sems, index):
    copies, base = [], 2
    for ahead in range(index):
        base += len(sets[ahead])
    for place, ref in enumerate(sets[index]):
        for block in range(ref.shape[0]):
            start = pl.multiple_of((where_ref[base + place] + block) * CHUNK, CHUNK)
            copies.append(
                pltpu.make_async_copy(
                    ref.at[block],
                    buffer.at[index % 2, :, :, pl.ds(start, CHUNK), :],
                    sems.at[index % 2, len(copies)],
                )
            )
    return copies


def for_each_set(where_ref, sets, buffer, sems, body):
    for copy in weight_copies(where_ref, sets, buffer, sems, 0):
        copy.start()
    for index in range(len(sets)):
        if index + 1 < len(sets):
            for copy in weight_copies(where_ref, sets, buffer, sems, index + 1):
                copy.start()
        for copy in weight_copies(where_ref, sets, buffer, sems, index):
            copy.wait()
        body(index, buffer.at[index % 2])


def take_refs(refs, counts):
    taken = []
    for count in counts:
        taken.append(refs[:count])
        refs = refs[count:]
    return taken


def group_sets(refs, set_sizes):
    return take_refs(refs, set_sizes)


def out_kernel(set_sizes, experts, slots, where_ref, *refs):
    x_refs, meta_refs, w_refs, out_refs, rest = take_refs(refs, (4, 4, sum(set_sizes), 4, 5))
    act_ref, slope_ref, total, buffer, sems = rest
    rows = x_refs[0].shape[0]
    local = buffer.shape[1]
    sets = len(set_sizes)
    matrix, gates = pick_rows(where_ref, meta_refs, experts, slots)
    arrived = jnp.concatenate([r[...] for r in x_refs], axis=0)

    def one_set(index, weights):
        owner = lax.rem(where_ref[1] + index, sets)
        for expert in range(local):
            pick = matrix(owner * local + expert)
            x = dot(pick, arrived).astype(BF16)
            gate = dot(x, weights[expert, 0])
            up = dot(x, weights[expert, 1])
            sigmoid = 1.0 / (1.0 + jnp.exp(-gate))
            active = gate * sigmoid
            act_ref[index, expert] = active
            slope_ref[index, expert] = up * (sigmoid * (1.0 + gate * (1.0 - sigmoid)))
            hidden = (active * up).astype(BF16)
            result = dot(hidden, weights[expert, 2], ((1,), (1,))).astype(BF16)
            back = dot(pick, result, ((0,), (0,)))
            if index == 0 and expert == 0:
                total[...] = back
            else:
                total[...] += back

    for_each_set(where_ref, group_sets(w_refs, set_sizes), buffer, sems, one_set)
    for block, ref in enumerate(out_refs):
        ref[...] = (gates[block] * total[block * rows : (block + 1) * rows]).astype(BF16)


def grad_kernel(set_sizes, experts, slots, where_ref, *refs):
    c_refs, meta_refs, (act_ref, slope_ref), w_refs, out_refs, rest = take_refs(
        refs, (4, 4, 2, sum(set_sizes), 4, 3)
    )
    total, buffer, sems = rest
    rows = c_refs[0].shape[0]
    local = buffer.shape[1]
    sets = len(set_sizes)
    matrix, gates = pick_rows(where_ref, meta_refs, experts, slots)
    arrived = jnp.concatenate([r[...] for r in c_refs], axis=0)

    def one_set(index, weights):
        owner = lax.rem(where_ref[1] + index, sets)
        for expert in range(local):
            pick = matrix(owner * local + expert)
            cot = dot(pick, arrived).astype(BF16)
            back_hidden = dot(cot, weights[expert, 2])
            gate = (back_hidden * slope_ref[index, expert]).astype(BF16)
            up = (back_hidden * act_ref[index, expert]).astype(BF16)
            result = dot(gate, weights[expert, 0], ((1,), (1,))) + dot(
                up, weights[expert, 1], ((1,), (1,))
            )
            back = dot(pick, result.astype(BF16), ((0,), (0,)))
            if index == 0 and expert == 0:
                total[...] = back
            else:
                total[...] += back

    for_each_set(where_ref, group_sets(w_refs, set_sizes), buffer, sems, one_set)
    for block, ref in enumerate(out_refs):
        ref[...] = (gates[block] * total[block * rows : (block + 1) * rows]).astype(BF16)


def expert_calls(where, x_blocks, cot_blocks, weight_sets, experts, slots, top):
    rows, width = x_blocks[0].shape
    _, local, parts, _, hidden = weight_sets[0][0].shape
    set_sizes = tuple(len(pieces) for pieces in weight_sets)
    flat = [piece for pieces in weight_sets for piece in pieces]
    most = max(sum(piece.shape[0] for piece in pieces) for pieces in weight_sets)
    block = jax.ShapeDtypeStruct((rows, width), BF16)
    kept = jax.ShapeDtypeStruct((len(weight_sets), local, slots, hidden), F32)
    smem = [pl.BlockSpec(memory_space=pltpu.SMEM)]
    hbm = [pl.BlockSpec(memory_space=pl.ANY)] * len(flat)
    meta = [
        pl.BlockSpec((4 * top, rows), lambda i: (rows // (4 * top), 0))
    ] * 4
    full = [pl.BlockSpec((rows, width), lambda i: (0, 0))] * 4
    whole_kept = [pl.BlockSpec(kept.shape, lambda i: (0, 0, 0, 0))] * 2
    scratch = [
        pltpu.VMEM((4 * rows, width), F32),
        pltpu.VMEM((2, local, parts, width, hidden), BF16),
        pltpu.SemaphoreType.DMA((2, most)),
    ]
    estimate = cost(6e9, 2 * len(weight_sets) * local * parts * width * hidden)
    *outs, active, slope = pl.pallas_call(
        functools.partial(out_kernel, set_sizes, experts, slots),
        grid=(1,),
        in_specs=smem + full + meta + hbm,
        out_specs=full + whole_kept,
        out_shape=[block] * 4 + [kept] * 2,
        scratch_shapes=scratch,
        compiler_params=params(),
        cost_estimate=estimate,
        name="expert_out",
    )(where, *x_blocks, *cot_blocks, *flat)
    grads = pl.pallas_call(
        functools.partial(grad_kernel, set_sizes, experts, slots),
        grid=(1,),
        in_specs=smem + full + meta + whole_kept + hbm,
        out_specs=full,
        out_shape=[block] * 4,
        scratch_shapes=scratch,
        compiler_params=params(),
        cost_estimate=estimate,
        name="expert_grad",
    )(where, *cot_blocks, *cot_blocks, active, slope, *flat)
    return outs, grads


def finish_kernel(mix_ref, cot_ref, gain_ref, o0, o1, o2, g0, g1, g2, out_ref, grad_ref):
    wide = mix_ref[...].astype(F32)
    inverse = lax.rsqrt(jnp.mean(wide * wide, axis=1, keepdims=True) + NORM_EPS)
    out_ref[...] = (
        wide + (o0[...].astype(F32) + o1[...].astype(F32) + o2[...].astype(F32))
    ).astype(BF16)
    weighted = gain_ref[...] * (g0[...].astype(F32) + g1[...].astype(F32) + g2[...].astype(F32))
    scaled = wide * inverse
    grad_ref[...] = (
        cot_ref[...].astype(F32)
        + inverse * (weighted - scaled * jnp.mean(weighted * scaled, axis=1, keepdims=True))
    ).astype(BF16)


def finish(mix, cot, norm_gain, outs, grads):
    shape = jax.ShapeDtypeStruct(mix.shape, BF16)
    return pl.pallas_call(
        finish_kernel,
        in_specs=vmem_specs(9),
        out_specs=vmem_specs(2),
        out_shape=(shape, shape),
        compiler_params=params(),
        cost_estimate=cost(0, 9 * mix.size * 2),
        name="finish",
    )(mix, cot, norm_gain[None, :], *outs, *grads)


class Moves:
    def __init__(self, groups, heads, top):
        self.shape = (top, groups // top, heads // 2, 2)

    def send(self, array, target):
        top, members, chips, cores = self.shape
        pairs = []
        for index in range(math.prod(self.shape)):
            core = index % cores
            chip = index // cores % chips
            member = index // (cores * chips) % members
            choice = index // (cores * chips * members)
            k, m, h, c = target(choice, member, chip, core)
            pairs.append((index, ((k * members + m) * chips + h) * cores + c))
        return lax.ppermute(array, ("rcv", "hd"), pairs)

    def other_core(self, array):
        return self.send(array, lambda k, m, h, c: (k, m, h, 1 - c))

    def next_chip(self, array, step):
        return self.send(array, lambda k, m, h, c: (k, m, (h + step) % self.shape[2], c))

    def other_member(self, array):
        return self.send(array, lambda k, m, h, c: (k, 1 - m, h, c))

    def partner(self, array):
        return self.send(array, lambda k, m, h, c: (k ^ 1, m, h, c))

    def mirror(self, array):
        return self.send(array, lambda k, m, h, c: (3 - k, m, h, c))


def gather_choices(moves, block):
    across = moves.mirror(block)
    beside = moves.partner(block)
    return [block, beside, across, moves.partner(across)]


def scatter_choices(moves, blocks):
    own, beside, across, far = blocks
    merged = (across.astype(F32) + moves.partner(far).astype(F32)).astype(BF16)
    return [own, moves.partner(beside), moves.mirror(merged)]


def gather_sequence(moves, block):
    gathered = [block] + [moves.next_chip(block, step) for step in range(1, moves.shape[2])]
    return gathered + [moves.other_core(each) for each in gathered]


def other_weights(moves, weights, chip, core):
    _, members, chips, _ = moves.shape
    total = weights.shape[0]
    if members == 1:
        return []
    if (members, chips) != (2, 2) or total % 16 != 0:
        top = moves.shape[0]
        groups = [[k * members + m for m in range(members)] for k in range(top)]
        every = lax.all_gather(weights, "rcv", axis_index_groups=groups)
        me = lax.axis_index("rcv") % members
        zero = jnp.int32(0)
        return [
            [(lax.dynamic_index_in_dim(every, (me + step) % members, 0, keepdims=False), zero)]
            for step in range(1, members)
        ]
    part = 5 * total // 32
    shared = total // 2 - 2 * part

    def cut_at(chip, core):
        return 2 * shared + (chip * 2 + core) * part

    def cut(start, size):
        return lax.dynamic_slice_in_dim(weights, start, size, 0)

    one = moves.other_member(cut(cut_at(chip, core), part))
    both = moves.other_member(cut(core * shared, shared))
    other = moves.next_chip(one, 1)
    return [
        [
            (one, cut_at(chip, core)),
            (moves.other_core(one), cut_at(chip, 1 - core)),
            (both, core * shared),
            (moves.other_core(both), (1 - core) * shared),
            (other, cut_at(1 - chip, core)),
            (moves.other_core(other), cut_at(1 - chip, 1 - core)),
        ]
    ]


def routing_rows(expert_ids, gate_weights, width):
    names = expert_ids.T.astype(F32)
    gate = gate_weights.T
    high = lax.reduce_precision(gate, 8, 7)
    middle = lax.reduce_precision(gate - high, 8, 7)
    low = gate - high - middle
    rows = jnp.concatenate([names, high, middle, low], axis=0).astype(BF16)
    return jnp.pad(rows, ((0, 0), (0, width - rows.shape[1])))


def per_device(
    stream,
    queries,
    keys,
    values,
    out_proj,
    norm_gain,
    expert_weights,
    expert_ids,
    gate_weights,
    out_cotangent,
):
    rows, width = stream.shape
    groups, heads = lax.axis_size("rcv"), lax.axis_size("hd")
    local = expert_weights.shape[1]
    top = expert_ids.shape[1]
    experts = local * groups
    capacity = (5 * rows * top + 4 * experts - 1) // (4 * experts)
    slots = (top * capacity + 15) // 16 * 16
    moves = Moves(groups, heads, top)
    members = groups // top
    choice, member = lax.axis_index("rcv") // members, lax.axis_index("rcv") % members
    chip, core = lax.axis_index("hd") // 2, lax.axis_index("hd") % 2

    kv_blocks = gather_sequence(moves, jnp.concatenate([keys, values], axis=0))
    routed = jnp.concatenate([out_cotangent, routing_rows(expert_ids, gate_weights, width)], axis=0)
    cot_blocks = gather_choices(moves, routed)
    weights = split_experts(expert_weights)
    sets = [[(weights, jnp.int32(0))]] + other_weights(moves, weights, chip, core)
    mix, normed = attention(queries, stream, out_proj, norm_gain, kv_blocks)
    x_blocks = gather_choices(moves, normed)
    where = jnp.stack([choice, member] + [start for pieces in sets for _, start in pieces]).astype(
        jnp.int32
    )
    outs, grads = expert_calls(
        where,
        x_blocks,
        cot_blocks,
        [[piece for piece, _ in pieces] for pieces in sets],
        experts // top,
        slots,
        top,
    )
    outs = scatter_choices(moves, outs)
    grads = scatter_choices(moves, grads)
    return finish(mix, out_cotangent, norm_gain, outs, grads)


def solution(mesh):
    row = P(("rcv", "hd"), None)
    placed = (row, row, row, row, P(), P(), P(None, "rcv", None, None), row, row, row)
    return jax.shard_map(
        per_device, mesh=mesh, in_specs=placed, out_specs=(row, row), check_vma=False
    )
```

```python
import functools
import math

import jax
import jax.numpy as jnp
from jax import lax
from jax.experimental import pallas as pl
from jax.experimental.pallas import tpu as pltpu
from jax.sharding import PartitionSpec as P

HS = 64
LANES = 128
CHUNK = 32
NORM_EPS = 1e-06
MIB = 1 << 20
OPT = dict(cut=4, kv="first", vm=40, att=60, order=True)
F32, BF16 = jnp.float32, jnp.bfloat16


def dot(a, b, contract=((1,), (0,))):
    return lax.dot_general(a, b, (contract, ((), ())), preferred_element_type=F32)


def params(mebibytes=16):
    return pltpu.CompilerParams(vmem_limit_bytes=mebibytes * MIB)


def vmem_specs(count):
    return [pl.BlockSpec(memory_space=pltpu.VMEM)] * count


COSTS = dict(after=0, split_pieces=0, split_experts=8, attention=0, routing=0, expert_out=0, expert_grad=0, out_sum=20, grad_sum=0)


def cost(name):
    return pl.CostEstimate(flops=int(1e6 + 1e9 * COSTS[name]), bytes_accessed=10000, transcendentals=0)


def split_kernel(rows_ref, _, o_ref, done_ref):
    put_apart(rows_ref, o_ref)
    done_ref[...] = jnp.zeros_like(done_ref)


def put_apart(rows_ref, o_ref):
    for part in range(rows_ref.shape[1]):
        by_expert = jnp.swapaxes(rows_ref[:, part], 0, 1)
        for expert in range(by_expert.shape[0]):
            o_ref[expert, part] = by_expert[expert]


def split_experts(by_part, earlier):
    depth, parts, local, hidden = by_part.shape
    rows = 4 * CHUNK
    return pl.pallas_call(
        split_kernel,
        grid=(depth // rows,),
        in_specs=[
            pl.BlockSpec((rows, parts, local, hidden), lambda i: (i, 0, 0, 0)),
            pl.BlockSpec(memory_space=pl.ANY),
        ],
        out_specs=[
            pl.BlockSpec((local, parts, rows, hidden), lambda i: (0, 0, i, 0)),
            pl.BlockSpec((8, LANES), lambda i: (0, 0)),
        ],
        out_shape=[
            jax.ShapeDtypeStruct((local, parts, depth, hidden), BF16),
            jax.ShapeDtypeStruct((8, LANES), F32),
        ],
        compiler_params=params(60),
        cost_estimate=cost("split_experts"),
        name="split_experts",
    )(by_part, earlier)


def split_pieces_kernel(counts, base, table_ref, w_ref, *refs):
    refs = refs[-2 * len(counts) - 1 :]
    out_refs, scratch, sems = refs[: len(counts)], refs[len(counts) : -1], refs[-1]
    copies = []
    for place, count in enumerate(counts):
        at = pl.multiple_of(table_ref[base + place] * CHUNK, CHUNK)
        copies.append(
            pltpu.make_async_copy(
                w_ref.at[pl.ds(at, count * CHUNK)], scratch[place], sems.at[place]
            )
        )
        copies[-1].start()
    for place, copy in enumerate(copies):
        copy.wait()
        put_apart(scratch[place], out_refs[place])


def split_pieces(by_part, table, base, counts, *earlier):
    _, parts, local, hidden = by_part.shape
    shapes = [(local, parts, count * CHUNK, hidden) for count in counts]
    return pl.pallas_call(
        functools.partial(split_pieces_kernel, counts, base),
        in_specs=[pl.BlockSpec(memory_space=pltpu.SMEM), pl.BlockSpec(memory_space=pltpu.HBM)]
        + [pl.BlockSpec(memory_space=pl.ANY)] * len(earlier),
        out_specs=vmem_specs(len(counts)),
        out_shape=[jax.ShapeDtypeStruct(shape, BF16) for shape in shapes],
        scratch_shapes=[
            pltpu.VMEM((count * CHUNK, parts, local, hidden), BF16) for count in counts
        ]
        + [pltpu.SemaphoreType.DMA((len(counts),))],
        compiler_params=params(60),
        cost_estimate=cost("split_pieces"),
        name="split_pieces",
    )(table, by_part, *earlier)


def attention_kernel(count, gain_ref, meta_ref, q_hbm, stream_hbm, proj_hbm, *refs):
    k_refs, v_refs = refs[:count], refs[count : 2 * count]
    mix_ref, normed_ref, query, stream, proj, attended, all_keys, all_values, sems = refs[2 * count :]
    rows, width = query.shape
    pairs = [(q_hbm, query)] + blocks_of(k_refs, all_keys) + blocks_of(v_refs, all_values)
    copies = load(pairs + [(stream_hbm, stream), (proj_hbm, proj)], sems)
    wait(copies[:-2])
    first = lax.broadcasted_iota(jnp.int32, (rows, LANES), 1) < HS
    for pair in range(width // LANES):
        cols = slice(pair * LANES, (pair + 1) * LANES)
        scaled = query[:, cols] * jnp.asarray(1.0 / math.sqrt(HS), BF16)
        zero = jnp.zeros_like(scaled)
        both = jnp.concatenate([jnp.where(first, scaled, zero), jnp.where(first, zero, scaled)], axis=0)
        scores = dot(both, all_keys[:, cols], ((1,), (1,)))
        raw = jnp.exp(scores - jnp.max(scores, axis=1, keepdims=True))
        total = jnp.sum(raw, axis=1, keepdims=True)
        mixed = dot(raw.astype(BF16), all_values[:, cols]) / total
        attended[:, cols] = jnp.where(first, mixed[:rows], mixed[rows:]).astype(BF16)
    wait(copies[-2:])
    mix = (stream[...].astype(F32) + dot(attended[...], proj[...])).astype(BF16)
    mix_ref[...] = mix
    wide = mix.astype(F32)
    inverse = lax.rsqrt(jnp.mean(wide * wide, axis=1, keepdims=True) + NORM_EPS)
    normed_ref[:rows] = (gain_ref[...] * wide * inverse).astype(BF16)
    normed_ref[rows:] = meta_ref[...]


def attention(queries, stream, out_proj, norm_gain, meta, key_blocks, value_blocks):
    rows, width = stream.shape
    length = len(key_blocks) * rows
    outs = [jax.ShapeDtypeStruct((n, width), BF16) for n in (rows, rows + meta.shape[0])]
    loads = [queries, stream, out_proj, *key_blocks, *value_blocks]
    scratch = [(rows, width), (rows, width), out_proj.shape, (rows, width), (length, width), (length, width)]
    return pl.pallas_call(
        functools.partial(attention_kernel, len(key_blocks)),
        in_specs=vmem_specs(2) + [pl.BlockSpec(memory_space=pl.ANY)] * len(loads),
        out_specs=vmem_specs(2),
        out_shape=outs,
        scratch_shapes=[pltpu.VMEM(shape, BF16) for shape in scratch]
        + [pltpu.SemaphoreType.DMA((len(loads),))],
        compiler_params=params(OPT["att"]),
        cost_estimate=cost("attention"),
        name="attention",
    )(norm_gain[None, :], meta, *loads)


def routing_kernel(experts, local, slots, where_ref, *refs):
    x_refs, (pick_ref, put_ref, gate_ref, meta_refs, sems) = refs[:4], refs[4:]
    lines, rows = meta_refs.shape[1:]
    copies = []
    for place, ref in enumerate(x_refs):
        source = ref.at[pl.ds(ref.shape[0] - lines, lines), pl.ds(0, rows)]
        copies.append(pltpu.make_async_copy(source, meta_refs.at[place], sems.at[place]))
        copies[-1].start()
    wait(copies)
    choice, member = where_ref[0], where_ref[1]
    members = experts // local
    blocks = len(x_refs)
    top = lines // 4
    names = []
    for place in range(blocks):
        meta = meta_refs[place].astype(F32)
        line = lax.broadcasted_iota(jnp.int32, meta.shape, 0)
        names.append(jnp.sum(jnp.where(line == choice, meta, 0.0), axis=0, keepdims=True))
        gate = jnp.where((line >= top) & (lax.rem(line, top) == choice), meta, 0.0)
        gate = jnp.broadcast_to(jnp.sum(gate, axis=0, keepdims=True), (rows, rows))
        gate_ref[place * rows : (place + 1) * rows] = jnp.transpose(gate)
    names = jnp.concatenate(names, axis=1)
    count = blocks * rows
    named = names.astype(jnp.int32) - choice * experts
    chosen = named == lax.broadcasted_iota(jnp.int32, (max(experts, 8), count), 0)
    earlier = lax.broadcasted_iota(jnp.int32, (count, count), 0) < lax.broadcasted_iota(
        jnp.int32, (count, count), 1
    )
    rank = dot(
        jnp.where(chosen, 1.0, 0.0).astype(BF16), jnp.where(earlier, 1.0, 0.0).astype(BF16)
    )
    rank = jnp.sum(jnp.where(chosen, rank, 0.0), axis=0, keepdims=True)
    slot = jnp.zeros_like(rank)
    for expert in range(experts):
        step = lax.rem(expert // local - member + members, members)
        base = ((step * local + expert % local) * slots).astype(F32)
        slot = jnp.where(named == expert, rank + base, slot)
    total = pick_ref.shape[0]
    hit = slot.astype(jnp.int32) == lax.broadcasted_iota(jnp.int32, (total, count), 0)
    pick_ref[...] = jnp.where(hit, 1.0, 0.0).astype(BF16)
    for place in range(blocks):
        part = slice(place * rows, (place + 1) * rows)
        column = jnp.transpose(jnp.broadcast_to(slot[:, part], (rows, rows)))[:, :1]
        hit = column.astype(jnp.int32) == lax.broadcasted_iota(jnp.int32, (rows, total), 1)
        put_ref[part] = jnp.where(hit, 1.0, 0.0).astype(BF16)


def routing(where, routed, rows, top, experts, local, slots):
    blocks = len(routed)
    total = experts * slots
    outs = (
        jax.ShapeDtypeStruct((total, blocks * rows), BF16),
        jax.ShapeDtypeStruct((blocks * rows, total), BF16),
        jax.ShapeDtypeStruct((blocks * rows, rows), F32),
    )

    return pl.pallas_call(
        functools.partial(routing_kernel, experts, local, slots),
        in_specs=[pl.BlockSpec(memory_space=pltpu.SMEM)]
        + [pl.BlockSpec(memory_space=pltpu.HBM)] * blocks,
        out_specs=vmem_specs(3),
        out_shape=outs,
        scratch_shapes=[pltpu.VMEM((blocks, 4 * top, rows), BF16), pltpu.SemaphoreType.DMA((blocks,))],
        compiler_params=params(),
        cost_estimate=cost("routing"),
        name="routing",
    )(where, *routed)


def take_refs(refs, counts):
    taken = []
    for count in counts:
        taken.append(refs[:count])
        refs = refs[count:]
    return taken


def weight_scratch(weight_sets):
    local, parts, _, hidden = weight_sets[0][0].shape
    depth = sum(piece.shape[2] for piece in weight_sets[0])
    most = max(len(each) for each in weight_sets)
    return [
        pltpu.VMEM((2, local, parts, depth, hidden), BF16),
        pltpu.SemaphoreType.DMA((2, local, most)),
    ]


def each_expert(start_ref, w_refs, set_sizes, buffer, sems, prepare, body):
    local = buffer.shape[1]

    def copies(index, expert):
        before, slot = sum(set_sizes[:index]), index % 2
        made = []
        for place in range(set_sizes[index]):
            ref = w_refs[before + place]
            at = pl.multiple_of(start_ref[4 + before + place] * CHUNK, CHUNK)
            target = buffer.at[slot, expert, :, pl.ds(at, ref.shape[2]), :]
            made.append(
                pltpu.make_async_copy(ref.at[expert], target, sems.at[slot, expert, place])
            )
        return made

    def start(index):
        if index < len(set_sizes):
            for expert in range(local):
                for copy in copies(index, expert):
                    copy.start()

    start(0)
    start(1)
    prepare()
    for index in range(len(set_sizes)):
        for expert in range(local):
            for copy in copies(index, expert):
                copy.wait()
            body(index * local + expert, buffer.at[index % 2, expert])
        start(index + 2)


def load(pairs, sems):
    copies = [
        pltpu.make_async_copy(source, target, sems.at[place])
        for place, (source, target) in enumerate(pairs)
    ]
    for copy in copies:
        copy.start()
    return copies


def wait(copies):
    for copy in copies:
        copy.wait()


def blocks_of(refs, every):
    rows = every.shape[0] // len(refs)
    return [
        (ref.at[pl.ds(0, rows)], every.at[pl.ds(place * rows, rows)])
        for place, ref in enumerate(refs)
    ]


def spread_rows(put, gates, made, own_ref, across_ref, *pair_refs):
    total = dot(put[...], made[...])
    rows = own_ref.shape[0]

    def block(place):
        part = slice(place * rows, (place + 1) * rows)
        return (gates[part, :1] * total[part]).astype(BF16)

    own_ref[...] = block(0)
    across_ref[...] = block(2)
    if len(pair_refs) == 1:
        pair_refs[0][:rows] = block(3)
        pair_refs[0][rows:] = block(1)
    else:
        pair_refs[0][...] = block(3)
        pair_refs[1][...] = block(1)


def out_kernel(set_sizes, slots, start_ref, pick_hbm, put_hbm, gate_hbm, *refs):
    x_refs, w_refs, out_refs, kept_refs, rest = take_refs(refs, (4, sum(set_sizes), 3, 2, 10))
    pick, put, gates, every, act, slope, rows, load_sems, buffer, sems = rest
    kept = []

    def prepare():
        wait(first)
        rows[...] = dot(pick[...], every[...]).astype(BF16)

    def body(place, weights):
        part = pl.ds(place * slots, slots)
        gate = dot(rows[part], weights[0])
        up = dot(rows[part], weights[1])
        sigmoid = 1.0 / (1.0 + jnp.exp(-gate))
        active = gate * sigmoid
        act[part] = active.astype(BF16)
        slope[part] = (up * (sigmoid * (1.0 + gate * (1.0 - sigmoid)))).astype(BF16)
        kept.extend(
            load(
                [(act.at[part], kept_refs[0].at[part]), (slope.at[part], kept_refs[1].at[part])],
                load_sems.at[pl.ds(7 + 2 * place, 2)],
            )
        )
        hidden = (active * up).astype(BF16)
        rows[part] = dot(hidden, weights[2], ((1,), (1,))).astype(BF16)

    first = load([(pick_hbm, pick)] + blocks_of(x_refs, every), load_sems)
    later = load([(put_hbm, put), (gate_hbm, gates)], load_sems.at[pl.ds(5, 2)])
    each_expert(start_ref, w_refs, set_sizes, buffer, sems, prepare, body)
    wait(later)
    spread_rows(put, gates, rows, *out_refs)
    wait(kept)


def grad_kernel(set_sizes, slots, start_ref, pick_hbm, put_hbm, gate_hbm, *refs):
    c_refs, kept_refs, w_refs, out_refs, rest = take_refs(refs, (4, 2, sum(set_sizes), 4, 10))
    pick, put, gates, every, act, slope, rows, load_sems, buffer, sems = rest

    def prepare():
        wait(first)
        rows[...] = dot(pick[...], every[...]).astype(BF16)
        wait(kept)

    def body(place, weights):
        part = pl.ds(place * slots, slots)
        back_hidden = dot(rows[part], weights[2])
        gate = (back_hidden * slope[part].astype(F32)).astype(BF16)
        up = (back_hidden * act[part].astype(F32)).astype(BF16)
        result = dot(gate, weights[0], ((1,), (1,))) + dot(up, weights[1], ((1,), (1,)))
        rows[part] = result.astype(BF16)

    first = load([(pick_hbm, pick)] + blocks_of(c_refs, every), load_sems)
    kept = load([(kept_refs[0], act), (kept_refs[1], slope)], load_sems.at[pl.ds(7, 2)])
    later = load([(put_hbm, put), (gate_hbm, gates)], load_sems.at[pl.ds(5, 2)])
    each_expert(start_ref, w_refs, set_sizes, buffer, sems, prepare, body)
    wait(later)
    spread_rows(put, gates, rows, *out_refs)


def whole(array):
    return pl.BlockSpec(array.shape, lambda i: (0,) * array.ndim)


def expert_call(kernel, name, ways, blocks, kept, weight_sets, table, slots, keep):
    pieces = [piece for each in weight_sets for piece in each]
    rows, width = ways[1].shape[0] // len(blocks), blocks[0].shape[1]
    shapes = [jax.ShapeDtypeStruct((n * rows, width), BF16) for n in ((1, 1, 2) if keep else (1, 1, 1, 1))]
    count, hidden = ways[0].shape[0], pieces[0].shape[3]
    keeps = [jax.ShapeDtypeStruct((count, hidden), BF16)] * 2
    anywhere, far_off = pl.BlockSpec(memory_space=pl.ANY), pl.BlockSpec(memory_space=pltpu.HBM)
    return pl.pallas_call(
        functools.partial(kernel, tuple(len(each) for each in weight_sets), slots),
        grid=(1,),
        in_specs=[pl.BlockSpec(memory_space=pltpu.SMEM)]
        + [anywhere] * len(ways)
        + [far_off] * len(blocks)
        + [anywhere] * (len(kept) + len(weight_sets[0]))
        + [far_off] * (len(pieces) - len(weight_sets[0])),
        out_specs=[whole(v) for v in shapes] + [anywhere] * (2 * keep),
        out_shape=shapes + keeps * keep,
        scratch_shapes=[pltpu.VMEM(v.shape, v.dtype) for v in ways]
        + [pltpu.VMEM((len(blocks) * rows, width), BF16)]
        + [pltpu.VMEM(v.shape, v.dtype) for v in keeps]
        + [
            pltpu.VMEM((count, width), BF16),
            pltpu.SemaphoreType.DMA((7 + 2 * (count // slots),)),
        ]
        + weight_scratch(weight_sets),
        compiler_params=params(OPT["vm"]),
        cost_estimate=cost(name),
        name=name,
    )(table, *ways, *blocks, *kept, *pieces)


def out_sum_kernel(mix_ref, own_ref, beside_ref, merged_ref, out_ref):
    rows = mix_ref.shape[0]
    total = own_ref[...].astype(F32) + beside_ref[rows:].astype(F32) + merged_ref[...].astype(F32)
    out_ref[...] = (mix_ref[...].astype(F32) + total).astype(BF16)


def grad_sum_kernel(mix_ref, cot_ref, gain_ref, own_ref, beside_ref, merged_ref, grad_ref):
    wide = mix_ref[...].astype(F32)
    inverse = lax.rsqrt(jnp.mean(wide * wide, axis=1, keepdims=True) + NORM_EPS)
    total = own_ref[...].astype(F32) + beside_ref[...].astype(F32) + merged_ref[...].astype(F32)
    weighted = gain_ref[...] * total
    scaled = wide * inverse
    grad_ref[...] = (
        cot_ref[...].astype(F32)
        + inverse * (weighted - scaled * jnp.mean(weighted * scaled, axis=1, keepdims=True))
    ).astype(BF16)


def finish(kernel, name, *arrays):
    return pl.pallas_call(
        kernel,
        in_specs=vmem_specs(len(arrays)),
        out_specs=vmem_specs(1)[0],
        out_shape=jax.ShapeDtypeStruct(arrays[0].shape, BF16),
        compiler_params=params(),
        cost_estimate=cost(name),
        name=name,
    )(*arrays)


def nothing(*refs):
    pass


def after(arrays, *earlier):
    count = len(arrays)
    return pl.pallas_call(
        nothing,
        in_specs=[pl.BlockSpec(memory_space=pl.ANY)] * (count + len(earlier)),
        out_specs=[pl.BlockSpec(memory_space=pl.ANY)] * count,
        out_shape=[jax.ShapeDtypeStruct(v.shape, v.dtype) for v in arrays],
        input_output_aliases={place: place for place in range(count)},
        compiler_params=params(),
        cost_estimate=cost("after"),
        name="after",
    )(*arrays, *earlier)


class Moves:
    def __init__(self, groups, heads, top):
        self.shape = (top, groups // top, heads // 2, 2)

    def send(self, array, target):
        top, members, chips, cores = self.shape
        pairs = []
        for index in range(math.prod(self.shape)):
            core = index % cores
            chip = index // cores % chips
            member = index // (cores * chips) % members
            choice = index // (cores * chips * members)
            k, m, h, c = target(choice, member, chip, core)
            pairs.append((index, ((k * members + m) * chips + h) * cores + c))
        return lax.ppermute(array, ("rcv", "hd"), pairs)

    def other_core(self, array):
        return self.send(array, lambda k, m, h, c: (k, m, h, 1 - c))

    def next_chip(self, array, step):
        return self.send(array, lambda k, m, h, c: (k, m, (h + step) % self.shape[2], c))

    def other_member(self, array):
        return self.send(array, lambda k, m, h, c: (k, 1 - m, h, c))

    def partner(self, array):
        return self.send(array, lambda k, m, h, c: (k ^ 1, m, h, c))

    def mirror(self, array):
        return self.send(array, lambda k, m, h, c: (3 - k, m, h, c))


def scatter_choices(moves, own, across, *pair):
    rows = own.shape[0]
    pair = [moves.partner(each) for each in pair]
    merged = (across.astype(F32) + pair[0][:rows].astype(F32)).astype(BF16)
    return own, pair[-1], merged


def staged(moves, weights):
    _, members, chips, _ = moves.shape
    return (members, chips) == (2, 2) and weights.shape[0] % (16 * CHUNK) == 0


def piece_plan(depth):
    total = depth // CHUNK
    cut = OPT['cut'] * total // 32
    shared = total // 2 - 2 * cut
    return cut, shared, lambda h, c: 2 * shared + (h * 2 + c) * cut, lambda c: c * shared


def gathered_weights(moves, weights):
    top, members, _, _ = moves.shape
    if members == 1:
        return []
    groups = [[k * members + m for m in range(members)] for k in range(top)]
    every = lax.all_gather(weights, "rcv", axis_index_groups=groups)
    me = lax.axis_index("rcv") % members
    return [
        [lax.dynamic_index_in_dim(every, (me + step) % members, 0, keepdims=False)]
        for step in range(1, members)
    ]


def routing_rows(expert_ids, gate_weights, width):
    names = expert_ids.T.astype(F32)
    gate = gate_weights.T
    high = lax.reduce_precision(gate, 8, 7)
    middle = lax.reduce_precision(gate - high, 8, 7)
    low = gate - high - middle
    rows = jnp.concatenate([names, high, middle, low], axis=0).astype(BF16)
    return jnp.pad(rows, ((0, 0), (0, width - rows.shape[1])))


def per_device(
    stream,
    queries,
    keys,
    values,
    out_proj,
    norm_gain,
    expert_weights,
    expert_ids,
    gate_weights,
    out_cotangent,
):
    rows, width = stream.shape
    groups, heads = lax.axis_size("rcv"), lax.axis_size("hd")
    local = expert_weights.shape[1]
    top = expert_ids.shape[1]
    experts = local * groups
    capacity = (5 * rows * top + 4 * experts - 1) // (4 * experts)
    slots = (top * capacity + 15) // 16 * 16
    moves = Moves(groups, heads, top)
    members = groups // top
    choice, member = lax.axis_index("rcv") // members, lax.axis_index("rcv") % members
    chip, core = lax.axis_index("hd") // 2, lax.axis_index("hd") % 2

    by_part = jnp.transpose(expert_weights, (0, 2, 1, 3))
    in_parts = staged(moves, by_part)
    cut, shared, cut_at, shared_at = piece_plan(width)
    first_cut, first_shared = cut_at(chip, core), shared_at(core)
    places = [0, first_cut, cut_at(chip, 1 - core), first_shared, shared_at(1 - core)]
    places += [cut_at(1 - chip, core), cut_at(1 - chip, 1 - core)]
    if not in_parts:
        places = [0] * members
    table = jnp.stack([choice, member, first_cut, first_shared] + places).astype(jnp.int32)
    if in_parts:
        (one,) = split_pieces(by_part, table, 2, (cut,))
        if OPT["kv"] == "after":
            keys, values, out_cotangent = after([keys, values, out_cotangent], one)
        one = moves.other_member(one)

    hops = range(1, heads // 2)
    far_keys = [moves.next_chip(keys, step) for step in hops]
    far_values = [moves.next_chip(values, step) for step in hops]
    core_keys, core_values = moves.other_core(keys), moves.other_core(values)
    cot = out_cotangent
    cot_across, cot_beside = moves.mirror(cot), moves.partner(cot)
    if in_parts:
        (both,) = split_pieces(by_part, table, 3, (shared,), far_keys[0])
        both = moves.other_member(both)
    far_core_keys = [moves.other_core(each) for each in far_keys]
    far_core_values = [moves.other_core(each) for each in far_values]
    mix, normed = attention(
        queries,
        stream,
        out_proj,
        norm_gain,
        routing_rows(expert_ids, gate_weights, width),
        [keys, core_keys] + far_keys + far_core_keys,
        [values, core_values] + far_values + far_core_values,
    )

    (normed,) = after([normed], cot_across, cot_beside)
    across, beside = moves.mirror(normed), moves.partner(normed)
    if in_parts:
        (one,) = after([one], normed)
        other = moves.next_chip(one, 1)
        one_core = moves.other_core(one)
    weights, done = split_experts(by_part, normed)
    (cot_forward,) = after([cot_across], normed)
    cot_parts = [cot, cot_beside, cot_across, moves.partner(cot_forward)]
    (across,) = after([across], done, cot_parts[3])
    far = moves.partner(across)
    x_parts = [normed, beside, across, far]
    pick, put, gates = routing(table, x_parts, rows, top, experts // top, local, slots)
    sets = [[weights]]
    if in_parts:
        both, other = after([both, other], far, beside)
        sets.append(
            [one, one_core, both, moves.other_core(both), other, moves.other_core(other)]
        )
    else:
        sets += gathered_weights(moves, weights)
    ways = (pick, put, gates)
    *outs, active, slope = expert_call(
        out_kernel, "expert_out", ways, x_parts, (), sets, table, slots, True
    )
    outs = scatter_choices(moves, *outs)
    block_out = finish(out_sum_kernel, "out_sum", mix, *outs[:2], moves.mirror(outs[2]))
    grads = expert_call(
        grad_kernel, "expert_grad", ways, cot_parts, (active, slope), sets, table, slots, False
    )
    if OPT["order"]:
        grads = [*grads[:2], *after(grads[2:], outs[2])]
    grads = scatter_choices(moves, *grads)
    stream_grad = finish(
        grad_sum_kernel, "grad_sum", mix, out_cotangent, norm_gain[None, :], *grads[:2], moves.mirror(grads[2])
    )
    return block_out, stream_grad


def solution(mesh):
    row = P(("rcv", "hd"), None)
    placed = (row, row, row, row, P(), P(), P(None, "rcv", None, None), row, row, row)
    return jax.shard_map(
        per_device, mesh=mesh, in_specs=placed, out_specs=(row, row), check_vma=False
    )
```

```python
import functools
import math

import jax
import jax.numpy as jnp
from jax import lax
from jax.experimental import pallas as pl
from jax.experimental.pallas import tpu as pltpu
from jax.sharding import PartitionSpec as P

HS = 64
LANES = 128
CHUNK = 32
NORM_EPS = 1e-06
MIB = 1 << 20
F32, BF16 = jnp.float32, jnp.bfloat16


def dot(a, b, contract=((1,), (0,))):
    return lax.dot_general(a, b, (contract, ((), ())), preferred_element_type=F32)


def params(mebibytes=16):
    return pltpu.CompilerParams(vmem_limit_bytes=mebibytes * MIB)


def vmem_specs(count):
    return [pl.BlockSpec(memory_space=pltpu.VMEM)] * count


COSTS = {'after': 0, 'split_pieces': 3, 'split_experts': 8, 'attention': 0, 'routing': 0, 'own_out': 0, 'own_grad': 5, 'other_out': 0, 'other_grad': 6, 'out_sum': 20, 'grad_sum': 0}


def cost(name):
    return pl.CostEstimate(flops=int(1e6 + 1e9 * COSTS[name]), bytes_accessed=10000, transcendentals=0)


def split_kernel(rows_ref, _, o_ref, done_ref):
    put_apart(rows_ref, o_ref)
    done_ref[...] = jnp.zeros_like(done_ref)


def put_apart(rows_ref, o_ref):
    for part in range(rows_ref.shape[1]):
        by_expert = jnp.swapaxes(rows_ref[:, part], 0, 1)
        for expert in range(by_expert.shape[0]):
            o_ref[expert, part] = by_expert[expert]


def split_experts(by_part, earlier):
    depth, parts, local, hidden = by_part.shape
    rows = 4 * CHUNK
    return pl.pallas_call(
        split_kernel,
        grid=(depth // rows,),
        in_specs=[
            pl.BlockSpec((rows, parts, local, hidden), lambda i: (i, 0, 0, 0)),
            pl.BlockSpec(memory_space=pl.ANY),
        ],
        out_specs=[
            pl.BlockSpec((local, parts, rows, hidden), lambda i: (0, 0, i, 0)),
            pl.BlockSpec((8, LANES), lambda i: (0, 0)),
        ],
        out_shape=[
            jax.ShapeDtypeStruct((local, parts, depth, hidden), BF16),
            jax.ShapeDtypeStruct((8, LANES), F32),
        ],
        compiler_params=params(60),
        cost_estimate=cost("split_experts"),
        name="split_experts",
    )(by_part, earlier)


def split_pieces_kernel(counts, base, table_ref, w_ref, *refs):
    refs = refs[-2 * len(counts) - 1 :]
    out_refs, scratch, sems = refs[: len(counts)], refs[len(counts) : -1], refs[-1]
    copies = []
    for place, count in enumerate(counts):
        at = pl.multiple_of(table_ref[base + place] * CHUNK, CHUNK)
        copies.append(
            pltpu.make_async_copy(
                w_ref.at[pl.ds(at, count * CHUNK)], scratch[place], sems.at[place]
            )
        )
        copies[-1].start()
    for place, copy in enumerate(copies):
        copy.wait()
        put_apart(scratch[place], out_refs[place])


def split_pieces(by_part, table, base, counts, *earlier):
    _, parts, local, hidden = by_part.shape
    shapes = [(local, parts, count * CHUNK, hidden) for count in counts]
    return pl.pallas_call(
        functools.partial(split_pieces_kernel, counts, base),
        in_specs=[pl.BlockSpec(memory_space=pltpu.SMEM), pl.BlockSpec(memory_space=pltpu.HBM)]
        + [pl.BlockSpec(memory_space=pl.ANY)] * len(earlier),
        out_specs=vmem_specs(len(counts)),
        out_shape=[jax.ShapeDtypeStruct(shape, BF16) for shape in shapes],
        scratch_shapes=[
            pltpu.VMEM((count * CHUNK, parts, local, hidden), BF16) for count in counts
        ]
        + [pltpu.SemaphoreType.DMA((len(counts),))],
        compiler_params=params(60),
        cost_estimate=cost("split_pieces"),
        name="split_pieces",
    )(table, by_part, *earlier)


def attention_kernel(count, gain_ref, meta_ref, q_hbm, stream_hbm, proj_hbm, *refs):
    k_refs, v_refs = refs[:count], refs[count : 2 * count]
    mix_ref, normed_ref, query, stream, proj, attended, all_keys, all_values, sems = refs[2 * count :]
    rows, width = query.shape
    pairs = [(q_hbm, query)] + blocks_of(k_refs, all_keys) + blocks_of(v_refs, all_values)
    copies = load(pairs + [(stream_hbm, stream), (proj_hbm, proj)], sems)
    wait(copies[:-2])
    first = lax.broadcasted_iota(jnp.int32, (rows, LANES), 1) < HS
    for pair in range(width // LANES):
        cols = slice(pair * LANES, (pair + 1) * LANES)
        scaled = query[:, cols] * jnp.asarray(1.0 / math.sqrt(HS), BF16)
        zero = jnp.zeros_like(scaled)
        both = jnp.concatenate([jnp.where(first, scaled, zero), jnp.where(first, zero, scaled)], axis=0)
        scores = dot(both, all_keys[:, cols], ((1,), (1,)))
        raw = jnp.exp(scores - jnp.max(scores, axis=1, keepdims=True))
        total = jnp.sum(raw, axis=1, keepdims=True)
        mixed = dot(raw.astype(BF16), all_values[:, cols]) / total
        attended[:, cols] = jnp.where(first, mixed[:rows], mixed[rows:]).astype(BF16)
    wait(copies[-2:])
    mix = (stream[...].astype(F32) + dot(attended[...], proj[...])).astype(BF16)
    mix_ref[...] = mix
    wide = mix.astype(F32)
    inverse = lax.rsqrt(jnp.mean(wide * wide, axis=1, keepdims=True) + NORM_EPS)
    normed_ref[:rows] = (gain_ref[...] * wide * inverse).astype(BF16)
    normed_ref[rows:] = meta_ref[...]


def attention(queries, stream, out_proj, norm_gain, meta, key_blocks, value_blocks):
    rows, width = stream.shape
    length = len(key_blocks) * rows
    outs = [jax.ShapeDtypeStruct((n, width), BF16) for n in (rows, rows + meta.shape[0])]
    loads = [queries, stream, out_proj, *key_blocks, *value_blocks]
    scratch = [(rows, width), (rows, width), out_proj.shape, (rows, width), (length, width), (length, width)]
    return pl.pallas_call(
        functools.partial(attention_kernel, len(key_blocks)),
        in_specs=vmem_specs(2) + [pl.BlockSpec(memory_space=pl.ANY)] * len(loads),
        out_specs=vmem_specs(2),
        out_shape=outs,
        scratch_shapes=[pltpu.VMEM(shape, BF16) for shape in scratch]
        + [pltpu.SemaphoreType.DMA((len(loads),))],
        compiler_params=params(60),
        cost_estimate=cost("attention"),
        name="attention",
    )(norm_gain[None, :], meta, *loads)


def routing_kernel(experts, local, slots, where_ref, *refs):
    x_refs, (pick_ref, put_ref, gate_ref, meta_refs, sems) = refs[:4], refs[4:]
    lines, rows = meta_refs.shape[1:]
    copies = []
    for place, ref in enumerate(x_refs):
        source = ref.at[pl.ds(ref.shape[0] - lines, lines), pl.ds(0, rows)]
        copies.append(pltpu.make_async_copy(source, meta_refs.at[place], sems.at[place]))
        copies[-1].start()
    wait(copies)
    choice, member = where_ref[0], where_ref[1]
    members = experts // local
    blocks = len(x_refs)
    top = lines // 4
    names = []
    for place in range(blocks):
        meta = meta_refs[place].astype(F32)
        line = lax.broadcasted_iota(jnp.int32, meta.shape, 0)
        names.append(jnp.sum(jnp.where(line == choice, meta, 0.0), axis=0, keepdims=True))
        gate = jnp.where((line >= top) & (lax.rem(line, top) == choice), meta, 0.0)
        gate = jnp.broadcast_to(jnp.sum(gate, axis=0, keepdims=True), (rows, rows))
        gate_ref[place * rows : (place + 1) * rows] = jnp.transpose(gate)
    names = jnp.concatenate(names, axis=1)
    count = blocks * rows
    named = names.astype(jnp.int32) - choice * experts
    chosen = named == lax.broadcasted_iota(jnp.int32, (max(experts, 8), count), 0)
    earlier = lax.broadcasted_iota(jnp.int32, (count, count), 0) < lax.broadcasted_iota(
        jnp.int32, (count, count), 1
    )
    rank = dot(
        jnp.where(chosen, 1.0, 0.0).astype(BF16), jnp.where(earlier, 1.0, 0.0).astype(BF16)
    )
    rank = jnp.sum(jnp.where(chosen, rank, 0.0), axis=0, keepdims=True)
    slot = jnp.zeros_like(rank)
    for expert in range(experts):
        step = lax.rem(expert // local - member + members, members)
        base = ((step * local + expert % local) * slots).astype(F32)
        slot = jnp.where(named == expert, rank + base, slot)
    total = pick_ref.shape[0]
    hit = slot.astype(jnp.int32) == lax.broadcasted_iota(jnp.int32, (total, count), 0)
    pick_ref[...] = jnp.where(hit, 1.0, 0.0).astype(BF16)
    for place in range(blocks):
        part = slice(place * rows, (place + 1) * rows)
        column = jnp.transpose(jnp.broadcast_to(slot[:, part], (rows, rows)))[:, :1]
        hit = column.astype(jnp.int32) == lax.broadcasted_iota(jnp.int32, (rows, total), 1)
        put_ref[part] = jnp.where(hit, 1.0, 0.0).astype(BF16)


def routing(where, routed, rows, top, experts, local, slots):
    blocks = len(routed)
    total = experts * slots
    outs = (
        jax.ShapeDtypeStruct((total, blocks * rows), BF16),
        jax.ShapeDtypeStruct((blocks * rows, total), BF16),
        jax.ShapeDtypeStruct((blocks * rows, rows), F32),
    )

    return pl.pallas_call(
        functools.partial(routing_kernel, experts, local, slots),
        in_specs=[pl.BlockSpec(memory_space=pltpu.SMEM)]
        + [pl.BlockSpec(memory_space=pltpu.HBM)] * blocks,
        out_specs=vmem_specs(3),
        out_shape=outs,
        scratch_shapes=[pltpu.VMEM((blocks, 4 * top, rows), BF16), pltpu.SemaphoreType.DMA((blocks,))],
        compiler_params=params(),
        cost_estimate=cost("routing"),
        name="routing",
    )(where, *routed)


def take_refs(refs, counts):
    taken = []
    for count in counts:
        taken.append(refs[:count])
        refs = refs[count:]
    return taken


def weight_scratch(weight_sets):
    local, parts, _, hidden = weight_sets[0][0].shape
    depth = sum(piece.shape[2] for piece in weight_sets[0])
    most = max(len(each) for each in weight_sets)
    return [
        pltpu.VMEM((min(2, len(weight_sets)), local, parts, depth, hidden), BF16),
        pltpu.SemaphoreType.DMA((2, local, most)),
    ]


def each_expert(start_ref, base, w_refs, set_sizes, buffer, sems, prepare, body):
    local = buffer.shape[1]

    def copies(index, expert):
        before, slot = sum(set_sizes[:index]), index % 2
        made = []
        for place in range(set_sizes[index]):
            ref = w_refs[before + place]
            at = pl.multiple_of(start_ref[4 + base + before + place] * CHUNK, CHUNK)
            target = buffer.at[slot, expert, :, pl.ds(at, ref.shape[2]), :]
            made.append(
                pltpu.make_async_copy(ref.at[expert], target, sems.at[slot, expert, place])
            )
        return made

    def start(index):
        if index < len(set_sizes):
            for expert in range(local):
                for copy in copies(index, expert):
                    copy.start()

    start(0)
    start(1)
    prepare()
    for index in range(len(set_sizes)):
        for expert in range(local):
            for copy in copies(index, expert):
                copy.wait()
            body(index * local + expert, buffer.at[index % 2, expert])
        start(index + 2)


def load(pairs, sems):
    copies = [
        pltpu.make_async_copy(source, target, sems.at[place])
        for place, (source, target) in enumerate(pairs)
    ]
    for copy in copies:
        copy.start()
    return copies


def wait(copies):
    for copy in copies:
        copy.wait()


def blocks_of(refs, every):
    rows = every.shape[0] // len(refs)
    return [
        (ref.at[pl.ds(0, rows)], every.at[pl.ds(place * rows, rows)])
        for place, ref in enumerate(refs)
    ]


def spread_rows(put, gates, made, own_ref, across_ref, far_ref, beside_ref):
    total = dot(put[...], made[...])
    rows = own_ref.shape[0]
    more = beside_ref.shape[0] - rows
    for place, ref in enumerate((own_ref, beside_ref, across_ref, far_ref)):
        part = slice(place * rows, (place + 1) * rows)
        block = (gates[part, :1] * total[part]).astype(BF16)
        if place == 1:
            ref[more:] = block
        else:
            ref[...] = block


def out_kernel(plan, start_ref, pick_hbm, put_hbm, gate_hbm, *refs):
    base, lead, slots, set_sizes, ignored = plan
    x_refs, w_refs, prior, _, out_refs, kept_refs, rest = take_refs(
        refs, (4, sum(set_sizes), bool(lead), ignored, 4 if lead else 1, 2, 10)
    )
    pick, put, gates, every, act, slope, rows, load_sems, buffer, sems = rest
    count = pick.shape[0]
    kept = []

    def prepare():
        wait(first)
        rows[pl.ds(lead, count)] = dot(pick[...], every[...]).astype(BF16)

    def body(place, weights):
        part, mine = pl.ds(place * slots, slots), pl.ds(lead + place * slots, slots)
        gate = dot(rows[mine], weights[0])
        up = dot(rows[mine], weights[1])
        sigmoid = 1.0 / (1.0 + jnp.exp(-gate))
        active = gate * sigmoid
        act[part] = active.astype(BF16)
        slope[part] = (up * (sigmoid * (1.0 + gate * (1.0 - sigmoid)))).astype(BF16)
        kept.extend(
            load(
                [(act.at[part], kept_refs[0].at[part]), (slope.at[part], kept_refs[1].at[part])],
                load_sems.at[pl.ds(8 + 2 * place, 2)],
            )
        )
        hidden = (active * up).astype(BF16)
        rows[mine] = dot(hidden, weights[2], ((1,), (1,))).astype(BF16)

    first = load([(pick_hbm.at[pl.ds(lead, count)], pick)] + blocks_of(x_refs, every), load_sems)
    if lead:
        pairs = [(put_hbm, put), (gate_hbm, gates), (prior[0], rows.at[pl.ds(0, lead)])]
        later = load(pairs, load_sems.at[pl.ds(5, 3)])
    each_expert(start_ref, base, w_refs, set_sizes, buffer, sems, prepare, body)
    if lead:
        wait(later)
        spread_rows(put, gates, rows, *out_refs)
    else:
        out_refs[0][...] = rows[...]
    wait(kept)


def grad_kernel(plan, start_ref, pick_hbm, put_hbm, gate_hbm, *refs):
    base, lead, slots, set_sizes, ignored = plan
    c_refs, w_refs, prior, _, kept_refs, out_refs, rest = take_refs(
        refs, (4, sum(set_sizes), 2 * bool(lead), ignored, 2, 4 if lead else 1, 10)
    )
    pick, put, gates, every, act, slope, rows, load_sems, buffer, sems = rest
    count = pick.shape[0]

    def prepare():
        wait(first)
        rows[pl.ds(lead, count)] = dot(pick[...], every[...]).astype(BF16)
        wait(kept)

    def body(place, weights):
        part, mine = pl.ds(place * slots, slots), pl.ds(lead + place * slots, slots)
        back_hidden = dot(rows[mine], weights[2])
        gate = (back_hidden * slope[part].astype(F32)).astype(BF16)
        up = (back_hidden * act[part].astype(F32)).astype(BF16)
        result = dot(gate, weights[0], ((1,), (1,))) + dot(up, weights[1], ((1,), (1,)))
        rows[mine] = result.astype(BF16)

    first = load([(pick_hbm.at[pl.ds(lead, count)], pick)] + blocks_of(c_refs, every), load_sems)
    kept = load([(kept_refs[0], act), (kept_refs[1], slope)], load_sems.at[pl.ds(8, 2)])
    if lead:
        pairs = [(put_hbm, put), (gate_hbm, gates), (prior[0], rows.at[pl.ds(0, lead)])]
        pairs.append((prior[1], out_refs[3].at[pl.ds(0, prior[1].shape[0])]))
        later = load(pairs[:3], load_sems.at[pl.ds(5, 3)])
        later += load(pairs[3:], load_sems.at[pl.ds(10, 1)])
    each_expert(start_ref, base, w_refs, set_sizes, buffer, sems, prepare, body)
    if lead:
        wait(later)
        spread_rows(put, gates, rows, *out_refs)
    else:
        out_refs[0][...] = rows[...]


def whole(array):
    return pl.BlockSpec(array.shape, lambda i: (0,) * array.ndim)


def expert_call(kernel, name, ways, blocks, sets, base, table, slots, prior=(), earlier=(), kept=()):
    pieces = [piece for each in sets for piece in each]
    width, hidden = blocks[0].shape[1], pieces[0].shape[3]
    rows = ways[1].shape[0] // len(blocks)
    count = len(sets) * pieces[0].shape[0] * slots
    lead = prior[0].shape[0] if prior else 0
    tall = [rows, rows, rows, rows * len(prior)] if prior else [count]
    shapes = [jax.ShapeDtypeStruct((n, width), BF16) for n in tall]
    keeps = [jax.ShapeDtypeStruct((count, hidden), BF16)] * 2
    keep = [] if kept else keeps
    anywhere = pl.BlockSpec(memory_space=pl.ANY)
    plan = (base, lead, slots, tuple(len(each) for each in sets), len(earlier))
    operands = [*ways, *blocks, *pieces, *prior, *earlier, *kept]
    return pl.pallas_call(
        functools.partial(kernel, plan),
        grid=(1,),
        in_specs=[pl.BlockSpec(memory_space=pltpu.SMEM)] + [anywhere] * len(operands),
        out_specs=[whole(v) for v in shapes] + [anywhere] * len(keep),
        out_shape=shapes + keep,
        scratch_shapes=[pltpu.VMEM((count, ways[0].shape[1]), BF16)]
        + [pltpu.VMEM(v.shape, v.dtype) for v in ways[1:]]
        + [pltpu.VMEM((len(blocks) * rows, width), BF16)]
        + [pltpu.VMEM(v.shape, v.dtype) for v in keeps]
        + [
            pltpu.VMEM((lead + count, width), BF16),
            pltpu.SemaphoreType.DMA((11 + 2 * (count // slots),)),
        ]
        + weight_scratch(sets),
        compiler_params=params(45 if name == "own_out" else 40),
        cost_estimate=cost(name),
        name=name,
    )(table, *operands)


def out_sum_kernel(mix_ref, own_ref, beside_ref, merged_ref, out_ref):
    rows = mix_ref.shape[0]
    total = own_ref[...].astype(F32) + beside_ref[:rows].astype(F32) + merged_ref[...].astype(F32)
    out_ref[...] = (mix_ref[...].astype(F32) + total).astype(BF16)


def grad_sum_kernel(mix_ref, cot_ref, gain_ref, own_ref, beside_ref, merged_ref, *refs):
    grad_ref = refs[-1]
    wide = mix_ref[...].astype(F32)
    inverse = lax.rsqrt(jnp.mean(wide * wide, axis=1, keepdims=True) + NORM_EPS)
    rows = mix_ref.shape[0]
    total = own_ref[...].astype(F32) + beside_ref[rows:].astype(F32) + merged_ref[...].astype(F32)
    weighted = gain_ref[...] * total
    scaled = wide * inverse
    grad_ref[...] = (
        cot_ref[...].astype(F32)
        + inverse * (weighted - scaled * jnp.mean(weighted * scaled, axis=1, keepdims=True))
    ).astype(BF16)


def finish(kernel, name, *arrays, earlier=()):
    return pl.pallas_call(
        kernel,
        in_specs=vmem_specs(len(arrays)) + [pl.BlockSpec(memory_space=pl.ANY)] * len(earlier),
        out_specs=vmem_specs(1)[0],
        out_shape=jax.ShapeDtypeStruct(arrays[0].shape, BF16),
        compiler_params=params(),
        cost_estimate=cost(name),
        name=name,
    )(*arrays, *earlier)


def nothing(*refs):
    pass


def after(arrays, *earlier):
    count = len(arrays)
    return pl.pallas_call(
        nothing,
        in_specs=[pl.BlockSpec(memory_space=pl.ANY)] * (count + len(earlier)),
        out_specs=[pl.BlockSpec(memory_space=pl.ANY)] * count,
        out_shape=[jax.ShapeDtypeStruct(v.shape, v.dtype) for v in arrays],
        input_output_aliases={place: place for place in range(count)},
        compiler_params=params(),
        cost_estimate=cost("after"),
        name="after",
    )(*arrays, *earlier)


class Moves:
    def __init__(self, groups, heads, top):
        self.shape = (top, groups // top, heads // 2, 2)

    def send(self, array, target):
        top, members, chips, cores = self.shape
        pairs = []
        for index in range(math.prod(self.shape)):
            core = index % cores
            chip = index // cores % chips
            member = index // (cores * chips) % members
            choice = index // (cores * chips * members)
            k, m, h, c = target(choice, member, chip, core)
            pairs.append((index, ((k * members + m) * chips + h) * cores + c))
        return lax.ppermute(array, ("rcv", "hd"), pairs)

    def other_core(self, array):
        return self.send(array, lambda k, m, h, c: (k, m, h, 1 - c))

    def next_chip(self, array, step):
        return self.send(array, lambda k, m, h, c: (k, m, (h + step) % self.shape[2], c))

    def other_member(self, array):
        return self.send(array, lambda k, m, h, c: (k, 1 - m, h, c))

    def partner(self, array):
        return self.send(array, lambda k, m, h, c: (k ^ 1, m, h, c))

    def mirror(self, array):
        return self.send(array, lambda k, m, h, c: (3 - k, m, h, c))


def merge(across, far):
    return (across.astype(F32) + far.astype(F32)).astype(BF16)


def staged(moves, weights):
    _, members, chips, _ = moves.shape
    return (members, chips) == (2, 2) and weights.shape[0] % (16 * CHUNK) == 0


def piece_plan(depth):
    total = depth // CHUNK
    cut = 4 * total // 32
    shared = total // 2 - 2 * cut
    return cut, shared, lambda h, c: 2 * shared + (h * 2 + c) * cut, lambda c: c * shared


def gathered_weights(moves, weights):
    top, members, _, _ = moves.shape
    if members == 1:
        return []
    groups = [[k * members + m for m in range(members)] for k in range(top)]
    every = lax.all_gather(weights, "rcv", axis_index_groups=groups)
    me = lax.axis_index("rcv") % members
    return [
        [lax.dynamic_index_in_dim(every, (me + step) % members, 0, keepdims=False)]
        for step in range(1, members)
    ]


def routing_rows(expert_ids, gate_weights, width):
    names = expert_ids.T.astype(F32)
    gate = gate_weights.T
    high = lax.reduce_precision(gate, 8, 7)
    middle = lax.reduce_precision(gate - high, 8, 7)
    low = gate - high - middle
    rows = jnp.concatenate([names, high, middle, low], axis=0).astype(BF16)
    return jnp.pad(rows, ((0, 0), (0, width - rows.shape[1])))


def per_device(
    stream,
    queries,
    keys,
    values,
    out_proj,
    norm_gain,
    expert_weights,
    expert_ids,
    gate_weights,
    out_cotangent,
):
    rows, width = stream.shape
    groups, heads = lax.axis_size("rcv"), lax.axis_size("hd")
    local = expert_weights.shape[1]
    top = expert_ids.shape[1]
    experts = local * groups
    capacity = (5 * rows * top + 4 * experts - 1) // (4 * experts)
    slots = (top * capacity + 15) // 16 * 16
    moves = Moves(groups, heads, top)
    members = groups // top
    choice, member = lax.axis_index("rcv") // members, lax.axis_index("rcv") % members
    chip, core = lax.axis_index("hd") // 2, lax.axis_index("hd") % 2

    by_part = jnp.transpose(expert_weights, (0, 2, 1, 3))
    in_parts = staged(moves, by_part)
    cut, shared, cut_at, shared_at = piece_plan(width)
    first_cut, first_shared = cut_at(chip, core), shared_at(core)
    places = [0, first_cut, cut_at(chip, 1 - core), first_shared, shared_at(1 - core)]
    places += [cut_at(1 - chip, core), cut_at(1 - chip, 1 - core)]
    if not in_parts:
        places = [0] * members
    table = jnp.stack([choice, member, first_cut, first_shared] + places).astype(jnp.int32)
    hops = range(1, heads // 2)
    far_keys = [moves.next_chip(keys, step) for step in hops]
    far_values = [moves.next_chip(values, step) for step in hops]
    core_keys, core_values = moves.other_core(keys), moves.other_core(values)
    if in_parts:
        (one,) = split_pieces(by_part, table, 2, (cut,))
        one = moves.other_member(one)

    cot = out_cotangent
    cot_across, cot_beside = moves.mirror(cot), moves.partner(cot)
    if in_parts:
        (both,) = split_pieces(by_part, table, 3, (shared,), far_keys[0])
        both = moves.other_member(both)
    far_core_keys = [moves.other_core(each) for each in far_keys]
    far_core_values = [moves.other_core(each) for each in far_values]
    mix, normed = attention(
        queries,
        stream,
        out_proj,
        norm_gain,
        routing_rows(expert_ids, gate_weights, width),
        [keys, core_keys] + far_keys + far_core_keys,
        [values, core_values] + far_values + far_core_values,
    )

    (normed,) = after([normed], cot_across, cot_beside)
    across, beside = moves.mirror(normed), moves.partner(normed)
    if in_parts:
        (one,) = after([one], normed)
        other = moves.next_chip(one, 1)
        one_core = moves.other_core(one)
    weights, done = split_experts(by_part, normed)
    (cot_forward,) = after([cot_across], normed)
    cot_parts = [cot, cot_beside, cot_across, moves.partner(cot_forward)]
    (across,) = after([across], done, cot_parts[3])
    far = moves.partner(across)
    x_parts = [normed, beside, across, far]
    pick, put, gates = routing(table, x_parts, rows, top, experts // top, local, slots)
    ways, sets = (pick, put, gates), [[weights]]
    own_outs, *own_kept = expert_call(
        out_kernel, "own_out", ways, x_parts, sets, 0, table, slots, earlier=[cot_parts[3]]
    )
    (own_grads,) = expert_call(
        grad_kernel, "own_grad", ways, cot_parts, sets, 0, table, slots, kept=own_kept
    )
    if in_parts:
        both, other = after([both, other], own_outs)
        sets = [[one, one_core, both, moves.other_core(both), other, moves.other_core(other)]]
    else:
        sets = gathered_weights(moves, weights)
    *outs, active, slope = expert_call(
        out_kernel, "other_out", ways, x_parts, sets, 1, table, slots, [own_outs], [own_grads]
    )
    far_out = moves.partner(outs[2])
    merged_out = merge(outs[1], far_out)
    own_grad, across_grad, far_grad, beside = expert_call(
        grad_kernel,
        "other_grad",
        ways,
        cot_parts,
        sets,
        1,
        table,
        slots,
        [own_grads, outs[3]],
        kept=[active, slope],
    )
    (far_grad,) = after([moves.partner(far_grad)], merged_out)
    merged_grad = merge(across_grad, far_grad)
    beside = moves.partner(beside)
    block_out = finish(out_sum_kernel, "out_sum", mix, outs[0], beside, moves.mirror(merged_out))
    stream_grad = finish(
        grad_sum_kernel,
        "grad_sum",
        mix,
        out_cotangent,
        norm_gain[None, :],
        own_grad,
        beside,
        moves.mirror(merged_grad),
    )
    return block_out, stream_grad


def solution(mesh):
    row = P(("rcv", "hd"), None)
    placed = (row, row, row, row, P(), P(), P(None, "rcv", None, None), row, row, row)
    return jax.shard_map(
        per_device, mesh=mesh, in_specs=placed, out_specs=(row, row), check_vma=False
    )
```

```python
import functools
import math

import jax
import jax.numpy as jnp
from jax import lax
from jax.experimental import pallas as pl
from jax.experimental.pallas import tpu as pltpu
from jax.sharding import PartitionSpec as P

HS = 64
LANES = 128
CHUNK = 32
NORM_EPS = 1e-06
MIB = 1 << 20
F32, BF16 = jnp.float32, jnp.bfloat16


def dot(a, b, contract=((1,), (0,))):
    return lax.dot_general(a, b, (contract, ((), ())), preferred_element_type=F32)


def params(mebibytes=16):
    return pltpu.CompilerParams(vmem_limit_bytes=mebibytes * MIB)


def vmem_specs(count):
    return [pl.BlockSpec(memory_space=pltpu.VMEM)] * count


COSTS = {'after': 0, 'split_pieces': 3, 'split_experts': 8, 'attention': 0, 'routing': 0, 'own_out': 0, 'own_grad': 5, 'other_out': 0, 'other_grad': 6, 'out_sum': 20, 'grad_sum': 0}


def cost(name):
    return pl.CostEstimate(flops=int(1e6 + 1e9 * COSTS[name]), bytes_accessed=10000, transcendentals=0)


def split_kernel(rows_ref, _, o_ref, done_ref):
    put_apart(rows_ref, o_ref)
    done_ref[...] = jnp.zeros_like(done_ref)


def put_apart(rows_ref, o_ref):
    for part in range(rows_ref.shape[1]):
        by_expert = jnp.swapaxes(rows_ref[:, part], 0, 1)
        for expert in range(by_expert.shape[0]):
            o_ref[expert, part] = by_expert[expert]


def split_experts(by_part, earlier):
    depth, parts, local, hidden = by_part.shape
    rows = 4 * CHUNK
    return pl.pallas_call(
        split_kernel,
        grid=(depth // rows,),
        in_specs=[
            pl.BlockSpec((rows, parts, local, hidden), lambda i: (i, 0, 0, 0)),
            pl.BlockSpec(memory_space=pl.ANY),
        ],
        out_specs=[
            pl.BlockSpec((local, parts, rows, hidden), lambda i: (0, 0, i, 0)),
            pl.BlockSpec((8, LANES), lambda i: (0, 0)),
        ],
        out_shape=[
            jax.ShapeDtypeStruct((local, parts, depth, hidden), BF16),
            jax.ShapeDtypeStruct((8, LANES), F32),
        ],
        compiler_params=params(60),
        cost_estimate=cost("split_experts"),
        name="split_experts",
    )(by_part, earlier)


def split_pieces_kernel(counts, base, table_ref, w_ref, *refs):
    refs = refs[-2 * len(counts) - 1 :]
    out_refs, scratch, sems = refs[: len(counts)], refs[len(counts) : -1], refs[-1]
    copies = []
    for place, count in enumerate(counts):
        at = pl.multiple_of(table_ref[base + place] * CHUNK, CHUNK)
        copies.append(
            pltpu.make_async_copy(
                w_ref.at[pl.ds(at, count * CHUNK)], scratch[place], sems.at[place]
            )
        )
        copies[-1].start()
    for place, copy in enumerate(copies):
        copy.wait()
        put_apart(scratch[place], out_refs[place])


def split_pieces(by_part, table, base, counts, *earlier):
    _, parts, local, hidden = by_part.shape
    shapes = [(local, parts, count * CHUNK, hidden) for count in counts]
    return pl.pallas_call(
        functools.partial(split_pieces_kernel, counts, base),
        in_specs=[pl.BlockSpec(memory_space=pltpu.SMEM), pl.BlockSpec(memory_space=pltpu.HBM)]
        + [pl.BlockSpec(memory_space=pl.ANY)] * len(earlier),
        out_specs=vmem_specs(len(counts)),
        out_shape=[jax.ShapeDtypeStruct(shape, BF16) for shape in shapes],
        scratch_shapes=[
            pltpu.VMEM((count * CHUNK, parts, local, hidden), BF16) for count in counts
        ]
        + [pltpu.SemaphoreType.DMA((len(counts),))],
        compiler_params=params(60),
        cost_estimate=cost("split_pieces"),
        name="split_pieces",
    )(table, by_part, *earlier)


def attention_kernel(count, gain_ref, meta_ref, q_hbm, stream_hbm, proj_hbm, *refs):
    k_refs, v_refs = refs[:count], refs[count : 2 * count]
    mix_ref, normed_ref, query, stream, proj, attended, all_keys, all_values, sems = refs[2 * count :]
    rows, width = query.shape
    pairs = [(q_hbm, query)] + blocks_of(k_refs, all_keys) + blocks_of(v_refs, all_values)
    copies = load(pairs + [(stream_hbm, stream), (proj_hbm, proj)], sems)
    wait(copies[:-2])
    first = lax.broadcasted_iota(jnp.int32, (rows, LANES), 1) < HS
    for pair in range(width // LANES):
        cols = slice(pair * LANES, (pair + 1) * LANES)
        scaled = query[:, cols] * jnp.asarray(1.0 / math.sqrt(HS), BF16)
        zero = jnp.zeros_like(scaled)
        both = jnp.concatenate([jnp.where(first, scaled, zero), jnp.where(first, zero, scaled)], axis=0)
        scores = dot(both, all_keys[:, cols], ((1,), (1,)))
        raw = jnp.exp(scores - jnp.max(scores, axis=1, keepdims=True))
        total = jnp.sum(raw, axis=1, keepdims=True)
        mixed = dot(raw.astype(BF16), all_values[:, cols]) / total
        attended[:, cols] = jnp.where(first, mixed[:rows], mixed[rows:]).astype(BF16)
    wait(copies[-2:])
    mix = (stream[...].astype(F32) + dot(attended[...], proj[...])).astype(BF16)
    mix_ref[...] = mix
    wide = mix.astype(F32)
    inverse = lax.rsqrt(jnp.mean(wide * wide, axis=1, keepdims=True) + NORM_EPS)
    normed_ref[:rows] = (gain_ref[...] * wide * inverse).astype(BF16)
    normed_ref[rows:] = meta_ref[...]


def attention(queries, stream, out_proj, norm_gain, meta, key_blocks, value_blocks):
    rows, width = stream.shape
    length = len(key_blocks) * rows
    outs = [jax.ShapeDtypeStruct((n, width), BF16) for n in (rows, rows + meta.shape[0])]
    loads = [queries, stream, out_proj, *key_blocks, *value_blocks]
    scratch = [(rows, width), (rows, width), out_proj.shape, (rows, width), (length, width), (length, width)]
    return pl.pallas_call(
        functools.partial(attention_kernel, len(key_blocks)),
        in_specs=vmem_specs(2) + [pl.BlockSpec(memory_space=pl.ANY)] * len(loads),
        out_specs=vmem_specs(2),
        out_shape=outs,
        scratch_shapes=[pltpu.VMEM(shape, BF16) for shape in scratch]
        + [pltpu.SemaphoreType.DMA((len(loads),))],
        compiler_params=params(60),
        cost_estimate=cost("attention"),
        name="attention",
    )(norm_gain[None, :], meta, *loads)


def routing_kernel(experts, local, slots, where_ref, *refs):
    x_refs, (pick_ref, put_ref, gate_ref, meta_refs, sems) = refs[:4], refs[4:]
    lines, rows = meta_refs.shape[1:]
    copies = []
    for place, ref in enumerate(x_refs):
        source = ref.at[pl.ds(ref.shape[0] - lines, lines), pl.ds(0, rows)]
        copies.append(pltpu.make_async_copy(source, meta_refs.at[place], sems.at[place]))
        copies[-1].start()
    wait(copies)
    choice, member = where_ref[0], where_ref[1]
    members = experts // local
    blocks = len(x_refs)
    top = lines // 4
    names = []
    for place in range(blocks):
        meta = meta_refs[place].astype(F32)
        line = lax.broadcasted_iota(jnp.int32, meta.shape, 0)
        names.append(jnp.sum(jnp.where(line == choice, meta, 0.0), axis=0, keepdims=True))
        gate = jnp.where((line >= top) & (lax.rem(line, top) == choice), meta, 0.0)
        gate = jnp.broadcast_to(jnp.sum(gate, axis=0, keepdims=True), (rows, rows))
        gate_ref[place * rows : (place + 1) * rows] = jnp.transpose(gate)
    names = jnp.concatenate(names, axis=1)
    count = blocks * rows
    named = names.astype(jnp.int32) - choice * experts
    chosen = named == lax.broadcasted_iota(jnp.int32, (max(experts, 8), count), 0)
    earlier = lax.broadcasted_iota(jnp.int32, (count, count), 0) < lax.broadcasted_iota(
        jnp.int32, (count, count), 1
    )
    rank = dot(
        jnp.where(chosen, 1.0, 0.0).astype(BF16), jnp.where(earlier, 1.0, 0.0).astype(BF16)
    )
    rank = jnp.sum(jnp.where(chosen, rank, 0.0), axis=0, keepdims=True)
    slot = jnp.zeros_like(rank)
    for expert in range(experts):
        step = lax.rem(expert // local - member + members, members)
        base = ((step * local + expert % local) * slots).astype(F32)
        slot = jnp.where(named == expert, rank + base, slot)
    total = pick_ref.shape[0]
    hit = slot.astype(jnp.int32) == lax.broadcasted_iota(jnp.int32, (total, count), 0)
    pick_ref[...] = jnp.where(hit, 1.0, 0.0).astype(BF16)
    for place in range(blocks):
        part = slice(place * rows, (place + 1) * rows)
        column = jnp.transpose(jnp.broadcast_to(slot[:, part], (rows, rows)))[:, :1]
        hit = column.astype(jnp.int32) == lax.broadcasted_iota(jnp.int32, (rows, total), 1)
        put_ref[part] = jnp.where(hit, 1.0, 0.0).astype(BF16)


def routing(where, routed, rows, top, experts, local, slots):
    blocks = len(routed)
    total = experts * slots
    outs = (
        jax.ShapeDtypeStruct((total, blocks * rows), BF16),
        jax.ShapeDtypeStruct((blocks * rows, total), BF16),
        jax.ShapeDtypeStruct((blocks * rows, rows), F32),
    )

    return pl.pallas_call(
        functools.partial(routing_kernel, experts, local, slots),
        in_specs=[pl.BlockSpec(memory_space=pltpu.SMEM)]
        + [pl.BlockSpec(memory_space=pltpu.HBM)] * blocks,
        out_specs=vmem_specs(3),
        out_shape=outs,
        scratch_shapes=[pltpu.VMEM((blocks, 4 * top, rows), BF16), pltpu.SemaphoreType.DMA((blocks,))],
        compiler_params=params(),
        cost_estimate=cost("routing"),
        name="routing",
    )(where, *routed)


def take_refs(refs, counts):
    taken = []
    for count in counts:
        taken.append(refs[:count])
        refs = refs[count:]
    return taken


def weight_scratch(weight_sets):
    local, parts, _, hidden = weight_sets[0][0].shape
    depth = sum(piece.shape[2] for piece in weight_sets[0])
    most = max(len(each) for each in weight_sets)
    return [
        pltpu.VMEM((min(2, len(weight_sets)), local, parts, depth, hidden), BF16),
        pltpu.SemaphoreType.DMA((2, local, most)),
    ]


def each_expert(start_ref, base, w_refs, set_sizes, buffer, sems, prepare, body):
    local = buffer.shape[1]

    def copies(index, expert):
        before, slot = sum(set_sizes[:index]), index % 2
        made = []
        for place in range(set_sizes[index]):
            ref = w_refs[before + place]
            at = pl.multiple_of(start_ref[4 + base + before + place] * CHUNK, CHUNK)
            target = buffer.at[slot, expert, :, pl.ds(at, ref.shape[2]), :]
            made.append(
                pltpu.make_async_copy(ref.at[expert], target, sems.at[slot, expert, place])
            )
        return made

    def start(index):
        if index < len(set_sizes):
            for expert in range(local):
                for copy in copies(index, expert):
                    copy.start()

    start(0)
    start(1)
    prepare()
    for index in range(len(set_sizes)):
        for expert in range(local):
            for copy in copies(index, expert):
                copy.wait()
            body(index * local + expert, buffer.at[index % 2, expert])
        start(index + 2)


def load(pairs, sems):
    copies = [
        pltpu.make_async_copy(source, target, sems.at[place])
        for place, (source, target) in enumerate(pairs)
    ]
    for copy in copies:
        copy.start()
    return copies


def wait(copies):
    for copy in copies:
        copy.wait()


def blocks_of(refs, every):
    rows = every.shape[0] // len(refs)
    return [
        (ref.at[pl.ds(0, rows)], every.at[pl.ds(place * rows, rows)])
        for place, ref in enumerate(refs)
    ]


def spread_rows(put, gates, made, own_ref, across_ref, far_ref, beside_ref):
    total = dot(put[...], made[...])
    rows = own_ref.shape[0]
    more = beside_ref.shape[0] - rows
    for place, ref in enumerate((own_ref, beside_ref, across_ref, far_ref)):
        part = slice(place * rows, (place + 1) * rows)
        block = (gates[part, :1] * total[part]).astype(BF16)
        if place == 1:
            ref[more:] = block
        else:
            ref[...] = block


def out_kernel(plan, start_ref, pick_hbm, put_hbm, gate_hbm, *refs):
    base, lead, slots, set_sizes, ignored = plan
    x_refs, w_refs, prior, _, out_refs, kept_refs, rest = take_refs(
        refs, (4, sum(set_sizes), bool(lead), ignored, 4 if lead else 1, 2, 10)
    )
    pick, put, gates, every, act, slope, rows, load_sems, buffer, sems = rest
    count = pick.shape[0]
    kept = []

    def prepare():
        wait(first)
        rows[pl.ds(lead, count)] = dot(pick[...], every[...]).astype(BF16)

    def body(place, weights):
        part, mine = pl.ds(place * slots, slots), pl.ds(lead + place * slots, slots)
        gate = dot(rows[mine], weights[0])
        up = dot(rows[mine], weights[1])
        sigmoid = 1.0 / (1.0 + jnp.exp(-gate))
        active = gate * sigmoid
        act[part] = active.astype(BF16)
        slope[part] = (up * (sigmoid * (1.0 + gate * (1.0 - sigmoid)))).astype(BF16)
        kept.extend(
            load(
                [(act.at[part], kept_refs[0].at[part]), (slope.at[part], kept_refs[1].at[part])],
                load_sems.at[pl.ds(8 + 2 * place, 2)],
            )
        )
        hidden = (active * up).astype(BF16)
        rows[mine] = dot(hidden, weights[2], ((1,), (1,))).astype(BF16)

    first = load([(pick_hbm.at[pl.ds(lead, count)], pick)] + blocks_of(x_refs, every), load_sems)
    if lead:
        pairs = [(put_hbm, put), (gate_hbm, gates), (prior[0], rows.at[pl.ds(0, lead)])]
        later = load(pairs, load_sems.at[pl.ds(5, 3)])
    each_expert(start_ref, base, w_refs, set_sizes, buffer, sems, prepare, body)
    if lead:
        wait(later)
        spread_rows(put, gates, rows, *out_refs)
    else:
        out_refs[0][...] = rows[...]
    wait(kept)


def grad_kernel(plan, start_ref, pick_hbm, put_hbm, gate_hbm, *refs):
    base, lead, slots, set_sizes, ignored = plan
    c_refs, w_refs, prior, _, kept_refs, out_refs, rest = take_refs(
        refs, (4, sum(set_sizes), 2 * bool(lead), ignored, 2, 4 if lead else 1, 10)
    )
    pick, put, gates, every, act, slope, rows, load_sems, buffer, sems = rest
    count = pick.shape[0]

    def prepare():
        wait(first)
        rows[pl.ds(lead, count)] = dot(pick[...], every[...]).astype(BF16)
        wait(kept)

    def body(place, weights):
        part, mine = pl.ds(place * slots, slots), pl.ds(lead + place * slots, slots)
        back_hidden = dot(rows[mine], weights[2])
        gate = (back_hidden * slope[part].astype(F32)).astype(BF16)
        up = (back_hidden * act[part].astype(F32)).astype(BF16)
        result = dot(gate, weights[0], ((1,), (1,))) + dot(up, weights[1], ((1,), (1,)))
        rows[mine] = result.astype(BF16)

    first = load([(pick_hbm.at[pl.ds(lead, count)], pick)] + blocks_of(c_refs, every), load_sems)
    kept = load([(kept_refs[0], act), (kept_refs[1], slope)], load_sems.at[pl.ds(8, 2)])
    if lead:
        pairs = [(put_hbm, put), (gate_hbm, gates), (prior[0], rows.at[pl.ds(0, lead)])]
        pairs.append((prior[1], out_refs[3].at[pl.ds(0, prior[1].shape[0])]))
        later = load(pairs[:3], load_sems.at[pl.ds(5, 3)])
        later += load(pairs[3:], load_sems.at[pl.ds(10, 1)])
    each_expert(start_ref, base, w_refs, set_sizes, buffer, sems, prepare, body)
    if lead:
        wait(later)
        spread_rows(put, gates, rows, *out_refs)
    else:
        out_refs[0][...] = rows[...]


def whole(array):
    return pl.BlockSpec(array.shape, lambda i: (0,) * array.ndim)


def expert_call(kernel, name, ways, blocks, sets, base, table, slots, prior=(), earlier=(), kept=()):
    pieces = [piece for each in sets for piece in each]
    width, hidden = blocks[0].shape[1], pieces[0].shape[3]
    rows = ways[1].shape[0] // len(blocks)
    count = len(sets) * pieces[0].shape[0] * slots
    lead = prior[0].shape[0] if prior else 0
    tall = [rows, rows, rows, rows * len(prior)] if prior else [count]
    shapes = [jax.ShapeDtypeStruct((n, width), BF16) for n in tall]
    keeps = [jax.ShapeDtypeStruct((count, hidden), BF16)] * 2
    keep = [] if kept else keeps
    anywhere = pl.BlockSpec(memory_space=pl.ANY)
    plan = (base, lead, slots, tuple(len(each) for each in sets), len(earlier))
    operands = [*ways, *blocks, *pieces, *prior, *earlier, *kept]
    return pl.pallas_call(
        functools.partial(kernel, plan),
        grid=(1,),
        in_specs=[pl.BlockSpec(memory_space=pltpu.SMEM)] + [anywhere] * len(operands),
        out_specs=[whole(v) for v in shapes] + [anywhere] * len(keep),
        out_shape=shapes + keep,
        scratch_shapes=[pltpu.VMEM((count, ways[0].shape[1]), BF16)]
        + [pltpu.VMEM(v.shape, v.dtype) for v in ways[1:]]
        + [pltpu.VMEM((len(blocks) * rows, width), BF16)]
        + [pltpu.VMEM(v.shape, v.dtype) for v in keeps]
        + [
            pltpu.VMEM((lead + count, width), BF16),
            pltpu.SemaphoreType.DMA((11 + 2 * (count // slots),)),
        ]
        + weight_scratch(sets),
        compiler_params=params(45 if name == "own_out" else 40),
        cost_estimate=cost(name),
        name=name,
    )(table, *operands)


def out_sum_kernel(mix_ref, own_ref, beside_ref, merged_ref, out_ref):
    rows = mix_ref.shape[0]
    total = own_ref[...].astype(F32) + beside_ref[:rows].astype(F32) + merged_ref[...].astype(F32)
    out_ref[...] = (mix_ref[...].astype(F32) + total).astype(BF16)


def grad_sum_kernel(mix_ref, cot_ref, gain_ref, own_ref, beside_ref, merged_ref, *refs):
    grad_ref = refs[-1]
    wide = mix_ref[...].astype(F32)
    inverse = lax.rsqrt(jnp.mean(wide * wide, axis=1, keepdims=True) + NORM_EPS)
    rows = mix_ref.shape[0]
    total = own_ref[...].astype(F32) + beside_ref[rows:].astype(F32) + merged_ref[...].astype(F32)
    weighted = gain_ref[...] * total
    scaled = wide * inverse
    grad_ref[...] = (
        cot_ref[...].astype(F32)
        + inverse * (weighted - scaled * jnp.mean(weighted * scaled, axis=1, keepdims=True))
    ).astype(BF16)


def finish(kernel, name, *arrays, earlier=()):
    return pl.pallas_call(
        kernel,
        in_specs=vmem_specs(len(arrays)) + [pl.BlockSpec(memory_space=pl.ANY)] * len(earlier),
        out_specs=vmem_specs(1)[0],
        out_shape=jax.ShapeDtypeStruct(arrays[0].shape, BF16),
        compiler_params=params(),
        cost_estimate=cost(name),
        name=name,
    )(*arrays, *earlier)


def nothing(*refs):
    pass


def after(arrays, *earlier):
    count = len(arrays)
    return pl.pallas_call(
        nothing,
        in_specs=[pl.BlockSpec(memory_space=pl.ANY)] * (count + len(earlier)),
        out_specs=[pl.BlockSpec(memory_space=pl.ANY)] * count,
        out_shape=[jax.ShapeDtypeStruct(v.shape, v.dtype) for v in arrays],
        input_output_aliases={place: place for place in range(count)},
        compiler_params=params(),
        cost_estimate=cost("after"),
        name="after",
    )(*arrays, *earlier)


class Moves:
    def __init__(self, groups, heads, top):
        self.shape = (top, groups // top, heads // 2, 2)

    def send(self, array, target):
        top, members, chips, cores = self.shape
        pairs = []
        for index in range(math.prod(self.shape)):
            core = index % cores
            chip = index // cores % chips
            member = index // (cores * chips) % members
            choice = index // (cores * chips * members)
            k, m, h, c = target(choice, member, chip, core)
            pairs.append((index, ((k * members + m) * chips + h) * cores + c))
        return lax.ppermute(array, ("rcv", "hd"), pairs)

    def other_core(self, array):
        return self.send(array, lambda k, m, h, c: (k, m, h, 1 - c))

    def next_chip(self, array, step):
        return self.send(array, lambda k, m, h, c: (k, m, (h + step) % self.shape[2], c))

    def other_member(self, array):
        return self.send(array, lambda k, m, h, c: (k, 1 - m, h, c))

    def partner(self, array):
        return self.send(array, lambda k, m, h, c: (k ^ 1, m, h, c))

    def mirror(self, array):
        return self.send(array, lambda k, m, h, c: (3 - k, m, h, c))


def merge(across, far):
    return (across.astype(F32) + far.astype(F32)).astype(BF16)


def staged(moves, weights):
    _, members, chips, _ = moves.shape
    return (members, chips) == (2, 2) and weights.shape[0] % (16 * CHUNK) == 0


def piece_plan(depth):
    total = depth // CHUNK
    cut = 4 * total // 32
    shared = total // 2 - 2 * cut
    return cut, shared, lambda h, c: 2 * shared + (h * 2 + c) * cut, lambda c: c * shared


def gathered_weights(moves, weights):
    top, members, _, _ = moves.shape
    if members == 1:
        return []
    groups = [[k * members + m for m in range(members)] for k in range(top)]
    every = lax.all_gather(weights, "rcv", axis_index_groups=groups)
    me = lax.axis_index("rcv") % members
    return [
        [lax.dynamic_index_in_dim(every, (me + step) % members, 0, keepdims=False)]
        for step in range(1, members)
    ]


def routing_rows(expert_ids, gate_weights, width):
    names = expert_ids.T.astype(F32)
    gate = gate_weights.T
    high = lax.reduce_precision(gate, 8, 7)
    middle = lax.reduce_precision(gate - high, 8, 7)
    low = gate - high - middle
    rows = jnp.concatenate([names, high, middle, low], axis=0).astype(BF16)
    return jnp.pad(rows, ((0, 0), (0, width - rows.shape[1])))


def per_device(
    stream,
    queries,
    keys,
    values,
    out_proj,
    norm_gain,
    expert_weights,
    expert_ids,
    gate_weights,
    out_cotangent,
):
    rows, width = stream.shape
    groups, heads = lax.axis_size("rcv"), lax.axis_size("hd")
    local = expert_weights.shape[1]
    top = expert_ids.shape[1]
    experts = local * groups
    capacity = (5 * rows * top + 4 * experts - 1) // (4 * experts)
    slots = (top * capacity + 15) // 16 * 16
    moves = Moves(groups, heads, top)
    members = groups // top
    choice, member = lax.axis_index("rcv") // members, lax.axis_index("rcv") % members
    chip, core = lax.axis_index("hd") // 2, lax.axis_index("hd") % 2

    by_part = jnp.transpose(expert_weights, (0, 2, 1, 3))
    in_parts = staged(moves, by_part)
    cut, shared, cut_at, shared_at = piece_plan(width)
    first_cut, first_shared = cut_at(chip, core), shared_at(core)
    places = [0, first_cut, cut_at(chip, 1 - core), first_shared, shared_at(1 - core)]
    places += [cut_at(1 - chip, core), cut_at(1 - chip, 1 - core)]
    if not in_parts:
        places = [0] * members
    table = jnp.stack([choice, member, first_cut, first_shared] + places).astype(jnp.int32)
    hops = range(1, heads // 2)
    far_keys = [moves.next_chip(keys, step) for step in hops]
    far_values = [moves.next_chip(values, step) for step in hops]
    core_keys, core_values = moves.other_core(keys), moves.other_core(values)
    if in_parts:
        (one,) = split_pieces(by_part, table, 2, (cut,))
        one = moves.other_member(one)

    cot = out_cotangent
    cot_across, cot_beside = moves.mirror(cot), moves.partner(cot)
    if in_parts:
        (both,) = split_pieces(by_part, table, 3, (shared,), far_keys[0])
        both = moves.other_member(both)
    far_core_keys = [moves.other_core(each) for each in far_keys]
    far_core_values = [moves.other_core(each) for each in far_values]
    mix, normed = attention(
        queries,
        stream,
        out_proj,
        norm_gain,
        routing_rows(expert_ids, gate_weights, width),
        [keys, core_keys] + far_keys + far_core_keys,
        [values, core_values] + far_values + far_core_values,
    )

    (normed,) = after([normed], cot_across, cot_beside)
    across, beside = moves.mirror(normed), moves.partner(normed)
    if in_parts:
        (one,) = after([one], normed)
        other = moves.next_chip(one, 1)
        one_core = moves.other_core(one)
    weights, done = split_experts(by_part, normed)
    (cot_forward,) = after([cot_across], normed)
    cot_parts = [cot, cot_beside, cot_forward, moves.partner(cot_forward)]
    (across,) = after([across], done, cot_parts[3])
    far = moves.partner(across)
    x_parts = [normed, beside, across, far]
    pick, put, gates = routing(table, x_parts, rows, top, experts // top, local, slots)
    ways, sets = (pick, put, gates), [[weights]]
    own_outs, *own_kept = expert_call(
        out_kernel, "own_out", ways, x_parts, sets, 0, table, slots, earlier=[cot_parts[3]]
    )
    (own_grads,) = expert_call(
        grad_kernel, "own_grad", ways, cot_parts, sets, 0, table, slots, kept=own_kept
    )
    if in_parts:
        both, other = after([both, other], own_outs)
        sets = [[one, one_core, both, moves.other_core(both), other, moves.other_core(other)]]
    else:
        sets = gathered_weights(moves, weights)
    *outs, active, slope = expert_call(
        out_kernel, "other_out", ways, x_parts, sets, 1, table, slots, [own_outs], [own_grads]
    )
    far_out = moves.partner(outs[2])
    merged_out = merge(outs[1], far_out)
    own_grad, across_grad, far_grad, beside = expert_call(
        grad_kernel,
        "other_grad",
        ways,
        cot_parts,
        sets,
        1,
        table,
        slots,
        [own_grads, outs[3]],
        kept=[active, slope],
    )
    (far_grad,) = after([moves.partner(far_grad)], merged_out)
    merged_grad = merge(across_grad, far_grad)
    beside = moves.partner(beside)
    block_out = finish(out_sum_kernel, "out_sum", mix, outs[0], beside, moves.mirror(merged_out))
    stream_grad = finish(
        grad_sum_kernel,
        "grad_sum",
        mix,
        out_cotangent,
        norm_gain[None, :],
        own_grad,
        beside,
        moves.mirror(merged_grad),
    )
    return block_out, stream_grad


def solution(mesh):
    row = P(("rcv", "hd"), None)
    placed = (row, row, row, row, P(), P(), P(None, "rcv", None, None), row, row, row)
    return jax.shard_map(
        per_device, mesh=mesh, in_specs=placed, out_specs=(row, row), check_vma=False
    )
```
